256 devices in a mesh: dom: 128 (over y, x, z), col: 2 (over core).
Axes of the slice: x: 4, y: 4, z: 8, core: 2. Of those that a mesh axis runs over, the one named last changes fastest.
Arguments:
- features: bfloat16 [131072, 256], P(('dom', 'col')), may hold values from -6 to 6
- weight: bfloat16 [256, 256], replicated, may hold values from -0.375 to 0.375
- cotangent: bfloat16 [131072, 256], P(('dom', 'col')), may hold values from -6 to 6
- tile_values: bfloat16 [10240, 128, 128], P(('dom', 'col')), may hold values from -0.15625 to 0.15625
- tile_rows: int32 [10240], P(('dom', 'col')), may hold values from 0 to 7
- tile_cols: int32 [10240], P(('dom', 'col')), may hold values from 0 to 131, as said below
- tile_count: int32 [256], P(('dom', 'col')), may hold values from 20 to 40, as said below
- send_blocks: int32 [256, 128], P(('dom', 'col')), may hold values from 0 to 3
Outputs:
- output_rows: bfloat16 [131072, 256], P(('dom', 'col'))
- feature_grad: bfloat16 [131072, 256], P(('dom', 'col'))
- weight_grad: float32 [256, 256], replicated
The draws below stay inside these ranges and needn't reach their ends.
Inputs may be any that keep to these rules, and one draw needn't show every extreme that they name: `tile_cols`: A value v below 4 names the device's own row block v; a value 4 + s names the row block that the device of partition s with the same col index sends to this partition; no receive slot is named by two tiles of one device. Only the first tile_count slots of a device's tiles are live; some device has all 40 live.
All inputs are finite; a program needn't handle non-finite values.
Results may differ from the reference program's by a relative error of at most 0.0049.
Values may be sent and summed in bfloat16 or wider, within the bound.
No kernel may reach another device: no remote copies, remote signals or barrier semaphores. Data moves between devices by JAX's collectives and lax.ppermute only.
A program may use at most 128 MiB of HBM per device.

```python
import jax
import jax.numpy as jnp
from jax import lax

F_IN = 256
F_OUT = 256
BLK = 128
NB = 8
TILES = 40
NODES = 131072
N_DOM = 128
N_COL = 2


def draw_tile_cols(key, part):
    devices_all = N_DOM * N_COL
    half_blocks = NB // N_COL
    remote_count = min(N_DOM, 3 * TILES // 4)
    slot_keys = jax.random.split(jax.random.fold_in(key, 11), devices_all)
    slot_perms = jax.vmap(lambda k: jax.random.permutation(k, N_DOM))(slot_keys)
    remote = slot_perms[:, :remote_count] + half_blocks
    local_ids = jax.random.randint(jax.random.fold_in(key, 12), (devices_all, TILES - remote_count), 0, half_blocks)
    joined = jnp.concatenate([remote.astype(jnp.int32), local_ids.astype(jnp.int32)], axis=1)
    order_keys = jax.random.split(jax.random.fold_in(key, 13), devices_all)
    orders = jax.vmap(lambda k: jax.random.permutation(k, TILES))(order_keys)
    placed = jnp.take_along_axis(joined, orders.astype(jnp.int32), axis=1)
    return placed.reshape(devices_all * TILES).astype(jnp.int32)


def draw_tile_count(key, part):
    devices_all = N_DOM * N_COL
    base = jax.random.randint(jax.random.fold_in(key, 21), (devices_all,), 0, TILES)
    skewed = TILES // 2 + base * base // (2 * TILES)
    picked = jax.random.randint(jax.random.fold_in(key, 22), (), 0, devices_all)
    return jnp.where(jnp.arange(devices_all) == picked, TILES, skewed).astype(jnp.int32)


def set_ends(entries, own_key, least, high):
    longest = entries.shape.index(max(entries.shape))
    spots = []
    for shift in (0, 1):
        where = [jax.random.randint(jax.random.fold_in(own_key, axis), (), 0, length) for axis, length in enumerate(entries.shape)]
        where[longest] = (where[longest] + shift) % entries.shape[longest]
        spots.append(tuple(where))
    return entries.at[spots[0]].set(least).at[spots[1]].set(high)


def levels(stream_key, shape, cuts, low, top_value):
    gain = 1.0
    for axis_at, shards_of in cuts:
        heights = jax.random.uniform(jax.random.fold_in(jax.random.fold_in(stream_key, 6), axis_at), (shards_of,), jnp.float32, low / len(cuts), top_value / len(cuts))
        gain = gain * jnp.repeat(jnp.exp(heights), shape[axis_at] // shards_of).reshape((-1,) + (1,) * (len(shape) - 1 - axis_at))
    return gain


def bell_draw(key, shape, scale, reach, cuts=(), held_as=jnp.bfloat16):
    array = jax.random.normal(key, shape, jnp.float32) * scale
    if len(cuts) > 0:
        array = levels(key, shape, cuts, -0.22, 0.18) * array
    return jnp.clip(array, min=-reach, max=reach).astype(held_as)


def setup_inputs(seed: int = 0) -> dict:
    key_list = jax.random.split(jax.random.key(seed), 9)
    features = bell_draw(key_list[0], (NODES, F_IN), 1.0, 6.0, ((0, 256),))
    weight = bell_draw(key_list[1], (F_IN, F_OUT), F_IN ** -0.5, 0.375)
    cotangent = bell_draw(key_list[2], (NODES, F_OUT), 1.0, 6.0, ((0, 256),))
    tile_values = bell_draw(key_list[3], (N_DOM * N_COL * TILES, BLK, BLK), (10 * BLK) ** -0.5, 0.15625, ((0, 256),))
    tile_rows = set_ends(jax.random.randint(key_list[4], (N_DOM * N_COL * TILES,), 0, NB), jax.random.fold_in(key_list[4], 1), 0, NB - 1).astype(jnp.int32)
    tile_cols = draw_tile_cols(jax.random.fold_in(key_list[8], 71), 0)
    tile_count = draw_tile_count(jax.random.fold_in(key_list[8], 71), 0)
    send_blocks = set_ends(jax.random.randint(key_list[7], (N_DOM * N_COL, N_DOM), 0, NB // N_COL), jax.random.fold_in(key_list[7], 1), 0, (NB // N_COL) - 1).astype(jnp.int32)
    return dict(features=features, weight=weight, cotangent=cotangent, tile_values=tile_values, tile_rows=tile_rows, tile_cols=tile_cols, tile_count=tile_count, send_blocks=send_blocks)


def reference(features, weight, cotangent, tile_values, tile_rows, tile_cols, tile_count, send_blocks):
    devices_all = N_DOM * N_COL
    half_blocks = NB // N_COL
    total_blocks = NB * N_DOM
    blocks = features.reshape(total_blocks, BLK, F_IN)
    tiles = tile_values.reshape(devices_all, TILES, BLK, BLK)
    rows_local = tile_rows.reshape(devices_all, TILES).astype(jnp.int32)
    cols_local = tile_cols.reshape(devices_all, TILES).astype(jnp.int32)
    device_ids = jnp.arange(devices_all, dtype=jnp.int32)
    part_ids = (device_ids // N_COL)[:, None]
    core_ids = (device_ids % N_COL)[:, None]
    slots = jnp.clip(cols_local - half_blocks, 0, N_DOM - 1).astype(jnp.int32)
    sender = (slots * N_COL + core_ids).astype(jnp.int32)
    sent_ids = send_blocks.astype(jnp.int32)[sender, jnp.broadcast_to(part_ids, sender.shape)]
    remote_block = slots * NB + core_ids * half_blocks + sent_ids
    own_block = part_ids * NB + core_ids * half_blocks + cols_local
    global_cols = jnp.where(cols_local < half_blocks, own_block, remote_block).astype(jnp.int32)
    global_rows = (part_ids * NB + rows_local).astype(jnp.int32)
    live_mask = (jnp.arange(TILES, dtype=jnp.int32)[None, :] < tile_count.astype(jnp.int32)[:, None]).astype(jnp.float32)

    def forward_step(carry, inputs):
        tile_block, live_row, row_ids, col_ids = inputs
        weighted = tile_block.astype(jnp.float32) * live_row[:, None, None]
        picked = blocks[col_ids].astype(jnp.float32)
        terms = jnp.einsum("tij,tjf->tif", weighted, picked, precision=lax.Precision.HIGHEST)
        return carry.at[row_ids].add(terms), None

    hidden_sum, _ = lax.scan(forward_step, jnp.zeros((total_blocks, BLK, F_IN), jnp.float32),
                             (tiles, live_mask, global_rows, global_cols))
    hidden = hidden_sum.astype(jnp.bfloat16).reshape(NODES, F_IN)
    output_rows = jnp.dot(hidden, weight, preferred_element_type=jnp.float32).astype(jnp.bfloat16)
    grad_hidden = lax.dot_general(cotangent, weight, (((1,), (1,)), ((), ())),
                                  preferred_element_type=jnp.float32).astype(jnp.bfloat16)
    grad_blocks = grad_hidden.reshape(total_blocks, BLK, F_IN)

    def backward_step(carry, inputs):
        tile_block, live_row, row_ids, col_ids = inputs
        weighted = tile_block.astype(jnp.float32) * live_row[:, None, None]
        picked = grad_blocks[row_ids].astype(jnp.float32)
        terms = jnp.einsum("tji,tjf->tif", weighted, picked, precision=lax.Precision.HIGHEST)
        return carry.at[col_ids].add(terms), None

    grad_sum, _ = lax.scan(backward_step, jnp.zeros((total_blocks, BLK, F_IN), jnp.float32),
                           (tiles, live_mask, global_rows, global_cols))
    feature_grad = grad_sum.astype(jnp.bfloat16).reshape(NODES, F_IN)
    weight_grad = lax.dot_general(hidden, cotangent, (((0,), (0,)), ((), ())),
                                  preferred_element_type=jnp.float32)
    weight_grad = weight_grad * jnp.float32(1.0 / (NODES ** 0.5))
    return output_rows, feature_grad, weight_grad
```

```python
import functools

import jax
import jax.numpy as jnp
from jax import lax
from jax.experimental import pallas as pl
from jax.experimental.pallas import tpu as pltpu
from jax.sharding import Mesh
from jax.sharding import PartitionSpec as P

PLANE = ("y", "x")
DOM = ("y", "x", "z")
SIZES = (4, 4, 8, 2)
BLK = 128
META = 16
VMEM_LIMIT = 60 * 2**20


def pack_kernel(cols, count, tiles, meta, out, tile_sem, meta_sem):
    groups, slots = out.shape[0], (out.shape[1] - META) // BLK

    def tile_copy(t):
        slot = jnp.maximum(cols[t] - 4, 0)
        d, z = lax.div(slot, slots), lax.rem(slot, slots)
        place = out.at[d, pl.ds(pl.multiple_of(z * BLK, BLK), BLK), :]
        return pltpu.make_async_copy(tiles.at[t], place, tile_sem.at[t])

    def start(t, carry):
        @pl.when(cols[t] >= 4)
        def _():
            tile_copy(t).start()

        return carry

    def finish(t, carry):
        @pl.when(cols[t] >= 4)
        def _():
            tile_copy(t).wait()

        return carry

    lax.fori_loop(0, count[0], start, 0)
    last = pltpu.make_async_copy(meta, out.at[:, pl.ds(slots * BLK, META), :], meta_sem)
    last.start()
    lax.fori_loop(0, count[0], finish, 0)
    last.wait()


def pack(cols, count, tiles, meta):
    groups, slots = 16, 8
    smem = pl.BlockSpec(memory_space=pltpu.SMEM)
    hbm = pl.BlockSpec(memory_space=pl.ANY)
    return pl.pallas_call(
        pack_kernel,
        out_shape=jax.ShapeDtypeStruct((groups, slots * BLK + META, BLK), tiles.dtype),
        in_specs=[smem, smem, hbm, hbm],
        out_specs=hbm,
        scratch_shapes=[pltpu.SemaphoreType.DMA((tiles.shape[0],)), pltpu.SemaphoreType.DMA],
        name="pack_tiles",
    )(cols, count, tiles, meta)


def rows_at(k):
    return pl.ds(pl.multiple_of(k * BLK, BLK), BLK)


def hidden_kernel(where, meta, ids, cols, rows, count, sent, feats, tiles, mine, peer, total, sem):
    half = total.shape[0] // 2
    c, z_me, r_me = where[0], where[1], where[2]

    def clear(i, carry):
        total[i] = jnp.zeros(total.shape[1:], total.dtype)
        return carry

    lax.fori_loop(0, 2 * half, clear, 0)

    def place(r, row):
        other = jnp.bitwise_xor(lax.div(row, 4), c)
        return other * half + r * 4 + lax.rem(row, 4)

    def remote(i, carry):
        r, z = lax.div(i, 8), lax.rem(i, 8)

        @pl.when(meta[i] > 0)
        def _():
            block = feats[z, rows_at(ids[z * 16 + r]), :]
            term = jnp.dot(sent[r, rows_at(z), :], block, preferred_element_type=jnp.float32)
            at = place(r, meta[i] - 1)
            total[at] = total[at] + term

        return carry

    lax.fori_loop(0, 128, remote, 0)

    def own(t, carry):
        @pl.when(cols[t] < 4)
        def _():
            block = feats[z_me, rows_at(jnp.minimum(cols[t], 3)), :]
            term = jnp.dot(tiles[t], block, preferred_element_type=jnp.float32)
            at = place(r_me, rows[t])
            total[at] = total[at] + term

        return carry

    lax.fori_loop(0, count[0], own, 0)
    copy = pltpu.make_async_copy(total.at[pl.ds(0, half)], mine, sem)
    copy.start()

    def cast(i, carry):
        peer[i] = total[half + i].astype(peer.dtype)
        return carry

    lax.fori_loop(0, half, cast, 0)
    copy.wait()


def hidden_parts(where, meta, ids, cols, rows, count, sent, feats, tiles):
    smem = pl.BlockSpec(memory_space=pltpu.SMEM)
    vmem = pl.BlockSpec(memory_space=pltpu.VMEM)
    width = feats.shape[2]
    return pl.pallas_call(
        hidden_kernel,
        out_shape=(
            jax.ShapeDtypeStruct((64, BLK, width), jnp.float32),
            jax.ShapeDtypeStruct((64, BLK, width), jnp.bfloat16),
        ),
        in_specs=[smem] * 6 + [vmem] * 3,
        out_specs=(pl.BlockSpec(memory_space=pl.ANY), vmem),
        scratch_shapes=[pltpu.VMEM((128, BLK, width), jnp.float32), pltpu.SemaphoreType.DMA],
        compiler_params=pltpu.CompilerParams(vmem_limit_bytes=VMEM_LIMIT),
        name="hidden_parts",
    )(where, meta, ids, cols, rows, count, sent, feats, tiles)


def grad_kernel(where, meta, ids, cols, rows, count, sent, grad_mine, grad_peer, tiles, out):
    c, z_me, r_me = where[0], where[1], where[2]

    def clear(i, carry):
        out[i] = jnp.zeros(out.shape[1:], out.dtype)
        return carry

    lax.fori_loop(0, out.shape[0], clear, 0)

    def add(at, tile, r, row):
        def go(source):
            term = lax.dot_general(
                tile, source[r * 4 + lax.rem(row, 4)], (((0,), (0,)), ((), ())),
                preferred_element_type=jnp.float32,
            )
            out[at] = out[at] + term

        @pl.when(lax.div(row, 4) == c)
        def _():
            go(grad_mine)

        @pl.when(lax.div(row, 4) != c)
        def _():
            go(grad_peer)

    def remote(i, carry):
        r, z = lax.div(i, 8), lax.rem(i, 8)

        @pl.when(meta[i] > 0)
        def _():
            add(z * 4 + ids[z * 16 + r], sent[r, rows_at(z), :], r, meta[i] - 1)

        return carry

    lax.fori_loop(0, 128, remote, 0)

    def own(t, carry):
        @pl.when(cols[t] < 4)
        def _():
            add(z_me * 4 + jnp.minimum(cols[t], 3), tiles[t], r_me, rows[t])

        return carry

    lax.fori_loop(0, count[0], own, 0)


def grad_parts(where, meta, ids, cols, rows, count, sent, grad_mine, grad_peer, tiles):
    smem = pl.BlockSpec(memory_space=pltpu.SMEM)
    vmem = pl.BlockSpec(memory_space=pltpu.VMEM)
    width = grad_mine.shape[2]
    return pl.pallas_call(
        grad_kernel,
        out_shape=jax.ShapeDtypeStruct((32, BLK, width), jnp.float32),
        in_specs=[smem] * 6 + [vmem] * 4,
        out_specs=vmem,
        compiler_params=pltpu.CompilerParams(vmem_limit_bytes=VMEM_LIMIT),
        name="grad_parts",
    )(where, meta, ids, cols, rows, count, sent, grad_mine, grad_peer, tiles)


def swap_cores(a):
    return lax.ppermute(a, "col", [(0, 1), (1, 0)])


def sum_everywhere(term, c):
    n = term.shape[1]
    halves = term.reshape(2, 128, n)
    keep = lax.dynamic_index_in_dim(halves, c, 0, keepdims=False)
    give = lax.dynamic_index_in_dim(halves, 1 - c, 0, keepdims=False)
    half = keep + swap_cores(give)
    rows = lax.all_to_all(half.reshape(128, 1, n), DOM, 0, 0, tiled=True)
    row = jnp.sum(rows, axis=0, keepdims=True)
    half = lax.all_to_all(jnp.broadcast_to(row, (128, 1, n)), DOM, 0, 0, tiled=True).reshape(128, n)
    other = swap_cores(half)
    first = jnp.where(c == 0, half, other)
    second = jnp.where(c == 0, other, half)
    return jnp.concatenate([first, second], axis=0)


def local(features, weight, cotangent, tile_values, tile_rows, tile_cols, tile_count, send_blocks):
    width = features.shape[1]
    node_total = features.shape[0] * lax.axis_size("col") * lax.axis_size(DOM)
    c = lax.axis_index("col")
    z_me = lax.axis_index("z")
    r_me = lax.axis_index(PLANE)
    where = jnp.stack([c, z_me, r_me]).astype(jnp.int32)

    ids_row = jnp.pad(send_blocks.astype(jnp.bfloat16), ((0, META - 1), (0, width - send_blocks.shape[1])))
    column = lax.all_gather(jnp.concatenate([features, ids_row], axis=0), "z", axis=0)
    own_grad = lax.dot_general(
        cotangent, weight, (((1,), (1,)), ((), ())), preferred_element_type=jnp.float32
    ).astype(jnp.bfloat16)
    grad_mine = lax.all_gather(own_grad.reshape(4, BLK, width), PLANE, axis=0, tiled=True)
    grad_peer = swap_cores(grad_mine)

    live = jnp.arange(tile_cols.shape[0], dtype=jnp.int32) < tile_count[0]
    slots = 4 + jnp.arange(128, dtype=jnp.int32)
    match = (tile_cols[:, None] == slots[None, :]) & live[:, None]
    slot_rows = jnp.sum(jnp.where(match, tile_rows[:, None] + 1, 0), axis=0)
    meta_rows = jnp.pad(
        slot_rows.astype(jnp.bfloat16).reshape(16, 1, 8), ((0, 0), (0, META - 1), (0, BLK - 8))
    )
    sent = lax.all_to_all(pack(tile_cols, tile_count, tile_values, meta_rows), PLANE, 0, 0, tiled=True)

    meta = sent[:, 8 * BLK, :8].astype(jnp.int32).reshape(128)
    ids = column[:, 4 * BLK, :128].astype(jnp.int32).reshape(8, 16, 8)
    ids = lax.dynamic_index_in_dim(ids, z_me, 2, keepdims=False).reshape(128)

    mine, peer = hidden_parts(where, meta, ids, tile_cols, tile_rows, tile_count, sent, column, tile_values)
    both = (mine + swap_cores(peer).astype(jnp.float32)).astype(jnp.bfloat16)
    parts = lax.all_to_all(both.reshape(16, 4 * BLK, width), PLANE, 0, 0, tiled=True)
    hidden = jnp.sum(parts.astype(jnp.float32), axis=0).astype(jnp.bfloat16)
    output_rows = jnp.dot(hidden, weight, preferred_element_type=jnp.float32).astype(jnp.bfloat16)
    local_weight = lax.dot_general(
        hidden, cotangent, (((0,), (0,)), ((), ())), preferred_element_type=jnp.float32
    ) * jnp.float32(1.0 / node_total**0.5)

    back = grad_parts(where, meta, ids, tile_cols, tile_rows, tile_count, sent, grad_mine, grad_peer, tile_values)
    grad_total = lax.psum_scatter(back.reshape(8, 4 * BLK, width), "z", scatter_dimension=0)
    feature_grad = grad_total.astype(jnp.bfloat16)
    weight_grad = sum_everywhere(local_weight, c)
    return (output_rows, feature_grad, weight_grad)


def solution(mesh):
    grid = Mesh(mesh.devices.reshape(SIZES), ("y", "x", "z", "col"))
    every = ("y", "x", "z", "col")
    return jax.shard_map(
        local,
        mesh=grid,
        in_specs=(
            P(every, None),
            P(),
            P(every, None),
            P(every, None, None),
            P(every),
            P(every),
            P(every),
            P(every, None),
        ),
        out_specs=(P(every, None), P(every, None), P()),
        check_vma=False,
    )
```

```python
import functools

import jax
import jax.numpy as jnp
from jax import lax
from jax.experimental import pallas as pl
from jax.experimental.pallas import tpu as pltpu
from jax.sharding import Mesh
from jax.sharding import PartitionSpec as P

PLANE = ("y", "x")
DOM = ("y", "x", "z")
SIZES = (4, 4, 8, 2)
BLK = 128
META = 16


def pack_kernel(cols, rows, count, tiles, out):
    slots = out.shape[1] // BLK
    here = pl.ds(slots * BLK, META)
    lane = lax.broadcasted_iota(jnp.int32, (META, BLK), 1)
    line = lax.broadcasted_iota(jnp.int32, (META, BLK), 0)

    def clear(d, carry):
        out[d, here, :] = jnp.zeros((META, BLK), out.dtype)
        return carry

    lax.fori_loop(0, out.shape[0], clear, 0)

    def one(t, carry):
        @pl.when(cols[t] >= 4)
        def _():
            slot = jnp.maximum(cols[t] - 4, 0)
            d, z = lax.div(slot, slots), lax.rem(slot, slots)
            out[d, rows_at(z), :] = tiles[t]
            mark = jnp.where((lane == z) & (line == 0), rows[t] + 1, 0)
            out[d, here, :] = (out[d, here, :].astype(jnp.float32) + mark.astype(jnp.float32)).astype(out.dtype)

        return carry

    lax.fori_loop(0, count[0], one, 0)


def pack(cols, rows, count, tiles):
    groups, slots = 16, 8
    smem = pl.BlockSpec(memory_space=pltpu.SMEM)
    vmem = pl.BlockSpec(memory_space=pltpu.VMEM)
    return pl.pallas_call(
        pack_kernel,
        out_shape=jax.ShapeDtypeStruct((groups, slots * BLK + META, BLK), tiles.dtype),
        in_specs=[smem, smem, smem, vmem],
        out_specs=vmem,
        compiler_params=pltpu.CompilerParams(vmem_limit_bytes=12 * 2**20),
        cost_estimate=cost(3),
        name="pack_tiles",
    )(cols, rows, count, tiles)


def cost(us):
    return pl.CostEstimate(flops=us * 10**6, bytes_accessed=us * 10**4, transcendentals=0)


def rows_at(k):
    return pl.ds(pl.multiple_of(k * BLK, BLK), BLK)


def hidden_kernel(first, where, meta, ids, cols, rows, count, sent, feats, tiles, *rest):
    out, total = rest[-2:]
    c, z_me, r_me = where[0], where[1], where[2]
    half = 1 - c if first else c

    def begin(i, carry):
        total[i] = jnp.zeros(total.shape[1:], total.dtype) if first else rest[0][i].astype(total.dtype)
        return carry

    lax.fori_loop(0, total.shape[0], begin, 0)

    def add(tile, block, r, row):
        at = r * 4 + lax.rem(row, 4)
        total[at] = total[at] + jnp.dot(tile, block, preferred_element_type=jnp.float32)

    def remote(i, carry):
        r, z = lax.div(i, 8), lax.rem(i, 8)
        row = meta[i] - 1

        @pl.when((meta[i] > 0) & (lax.div(row, 4) == half))
        def _():
            add(sent[r, rows_at(z), :], feats[z, rows_at(ids[z * 16 + r]), :], r, row)

        return carry

    lax.fori_loop(0, 128, remote, 0)

    def own(t, carry):
        @pl.when((cols[t] < 4) & (lax.div(rows[t], 4) == half))
        def _():
            add(tiles[t], feats[z_me, rows_at(jnp.minimum(cols[t], 3)), :], r_me, rows[t])

        return carry

    lax.fori_loop(0, count[0], own, 0)

    def cast(i, carry):
        out[i] = total[i].astype(out.dtype)
        return carry

    lax.fori_loop(0, total.shape[0], cast, 0)


def hidden_parts(where, meta, ids, cols, rows, count, sent, feats, tiles, *arrived):
    smem = pl.BlockSpec(memory_space=pltpu.SMEM)
    vmem = pl.BlockSpec(memory_space=pltpu.VMEM)
    width = feats.shape[2]
    return pl.pallas_call(
        functools.partial(hidden_kernel, not arrived),
        out_shape=jax.ShapeDtypeStruct((64, BLK, width), jnp.bfloat16),
        in_specs=[smem] * 6 + [vmem] * (3 + len(arrived)),
        out_specs=vmem,
        scratch_shapes=[pltpu.VMEM((64, BLK, width), jnp.float32)],
        compiler_params=pltpu.CompilerParams(vmem_limit_bytes=28 * 2**20),
        cost_estimate=cost(10),
        name="hidden_sums" if arrived else "hidden_for_other_core",
    )(where, meta, ids, cols, rows, count, sent, feats, tiles, *arrived)


def add_grads(half, where, meta, ids, cols, rows, count, sent, grads, tiles, total):
    z_me, r_me = where[1], where[2]

    def add(at, tile, r, row):
        term = lax.dot_general(
            tile, grads[r * 4 + lax.rem(row, 4)], (((0,), (0,)), ((), ())), preferred_element_type=jnp.float32
        )
        total[at] = total[at] + term

    def remote(i, carry):
        r, z = lax.div(i, 8), lax.rem(i, 8)
        row = meta[i] - 1

        @pl.when((meta[i] > 0) & (lax.div(row, 4) == half))
        def _():
            step = jnp.bitwise_and(z - z_me + 8, 7)
            add(step * 4 + ids[z * 16 + r], sent[r, rows_at(z), :], r, row)

        return carry

    lax.fori_loop(0, 128, remote, 0)

    def own(t, carry):
        @pl.when((cols[t] < 4) & (lax.div(rows[t], 4) == half))
        def _():
            add(jnp.minimum(cols[t], 3), tiles[t], r_me, rows[t])

        return carry

    lax.fori_loop(0, count[0], own, 0)


def grad_kernel(where, meta, ids, cols, rows, count, sent, mine, peer, tiles, *outs):
    total = outs[-1]

    def begin(i, carry):
        total[i] = jnp.zeros(total.shape[1:], total.dtype)
        return carry

    lax.fori_loop(0, total.shape[0], begin, 0)
    add_grads(where[0], where, meta, ids, cols, rows, count, sent, mine, tiles, total)
    add_grads(1 - where[0], where, meta, ids, cols, rows, count, sent, peer, tiles, total)
    for k in range(4):
        outs[0][rows_at(k), :] = total[k]
    for step in range(1, 8):
        for k in range(4):
            outs[step][rows_at(k), :] = total[step * 4 + k].astype(outs[step].dtype)


def grad_parts(where, meta, ids, cols, rows, count, sent, mine, peer, tiles):
    smem = pl.BlockSpec(memory_space=pltpu.SMEM)
    vmem = pl.BlockSpec(memory_space=pltpu.VMEM)
    width = mine.shape[2]
    return pl.pallas_call(
        grad_kernel,
        out_shape=[jax.ShapeDtypeStruct((4 * BLK, width), jnp.float32)]
        + [jax.ShapeDtypeStruct((4 * BLK, width), jnp.bfloat16)] * 7,
        in_specs=[smem] * 6 + [vmem] * 4,
        out_specs=[vmem] * 8,
        scratch_shapes=[pltpu.VMEM((32, BLK, width), jnp.float32)],
        compiler_params=pltpu.CompilerParams(vmem_limit_bytes=28 * 2**20),
        cost_estimate=cost(8),
        name="grad_sums",
    )(where, meta, ids, cols, rows, count, sent, mine, peer, tiles)


def term_kernel(scale, parts, cots, term):
    term[...] = jnp.zeros(term.shape, term.dtype)

    def product(i, carry):
        term[...] += lax.dot_general(
            parts[i], cots[i], (((0,), (0,)), ((), ())), preferred_element_type=jnp.float32
        )
        return carry

    lax.fori_loop(0, parts.shape[0], product, 0)
    term[...] = term[...] * scale


def weight_term(parts, cots, scale):
    vmem = pl.BlockSpec(memory_space=pltpu.VMEM)
    width = parts.shape[2]
    return pl.pallas_call(
        functools.partial(term_kernel, scale),
        out_shape=jax.ShapeDtypeStruct((width, width), jnp.float32),
        in_specs=[vmem] * 2,
        out_specs=vmem,
        compiler_params=pltpu.CompilerParams(vmem_limit_bytes=12 * 2**20),
        cost_estimate=cost(8),
        name="weight_term",
    )(parts, cots)


def output_kernel(parts, weight, *rest):
    output = rest[-1]
    total = parts[0].astype(jnp.float32)
    for i in range(1, parts.shape[0]):
        total = total + parts[i].astype(jnp.float32)
    hidden = total.astype(jnp.bfloat16)
    output[...] = jnp.dot(hidden, weight[...], preferred_element_type=jnp.float32).astype(output.dtype)


def output_from(parts, weight, *after):
    vmem = pl.BlockSpec(memory_space=pltpu.VMEM)
    return pl.pallas_call(
        output_kernel,
        out_shape=jax.ShapeDtypeStruct(parts.shape[1:], jnp.bfloat16),
        in_specs=[vmem] * 2 + [pl.BlockSpec(memory_space=pl.ANY)] * len(after),
        out_specs=vmem,
        compiler_params=pltpu.CompilerParams(vmem_limit_bytes=16 * 2**20),
        cost_estimate=cost(4),
        name="output_rows",
    )(parts, weight, *after)


def feature_kernel(own, *rest):
    weight, out = rest[-2:]
    total = own[...]
    for part in rest[:-2]:
        total = total + part[...].astype(jnp.float32)
    high = total.astype(jnp.bfloat16)
    low = (total - high.astype(jnp.float32)).astype(jnp.bfloat16)
    dims = (((1,), (1,)), ((), ()))
    grad = lax.dot_general(high, weight[...], dims, preferred_element_type=jnp.float32)
    grad = grad + lax.dot_general(low, weight[...], dims, preferred_element_type=jnp.float32)
    out[...] = grad.astype(out.dtype)


def feature_from(own, parts, weight):
    vmem = pl.BlockSpec(memory_space=pltpu.VMEM)
    return pl.pallas_call(
        feature_kernel,
        out_shape=jax.ShapeDtypeStruct(own.shape, jnp.bfloat16),
        in_specs=[vmem] * (2 + len(parts)),
        out_specs=vmem,
        compiler_params=pltpu.CompilerParams(vmem_limit_bytes=16 * 2**20),
        cost_estimate=cost(4),
        name="feature_gradient",
    )(own, *parts, weight)


def later_kernel(array, after, out):
    del after
    out[...] = array[...]


def later(array, after):
    vmem = pl.BlockSpec(memory_space=pltpu.VMEM)
    return pl.pallas_call(
        later_kernel,
        out_shape=jax.ShapeDtypeStruct(array.shape, array.dtype),
        in_specs=[vmem, pl.BlockSpec(memory_space=pl.ANY)],
        out_specs=vmem,
        compiler_params=pltpu.CompilerParams(vmem_limit_bytes=4 * 2**20),
        cost_estimate=cost(1),
        name="in_order",
    )(array, after)


def same_later_kernel(array, after, out):
    del array, after, out


def same_later(array, after):
    hbm = pl.BlockSpec(memory_space=pl.ANY)
    return pl.pallas_call(
        same_later_kernel,
        out_shape=jax.ShapeDtypeStruct(array.shape, array.dtype),
        in_specs=[hbm, hbm],
        out_specs=hbm,
        input_output_aliases={0: 0},
        cost_estimate=cost(1),
        name="in_order_in_place",
    )(array, after)


def swap_cores(a):
    return lax.ppermute(a, "col", [(0, 1), (1, 0)])


def sum_four(a, axis):
    me = lax.axis_index(axis)
    from_step = [a] + [lax.ppermute(a, axis, [(i, (i + step) % 4) for i in range(4)]) for step in (1, 2, 3)]
    total = None
    for source in range(4):
        step = jnp.bitwise_and(me - source + 4, 3)
        low = jnp.where(step == 0, from_step[0], from_step[1])
        high = jnp.where(step == 2, from_step[2], from_step[3])
        part = jnp.where(step < 2, low, high)
        total = part if total is None else total + part
    return total


def sum_everywhere(term, c, after):
    halves = term.reshape(2, 128, term.shape[1])
    keep = lax.dynamic_index_in_dim(halves, c, 0, keepdims=False)
    give = lax.dynamic_index_in_dim(halves, 1 - c, 0, keepdims=False)
    half = keep + swap_cores(give)
    for step in (1, 2, 4):
        half = half + lax.ppermute(half, "z", [(i, i ^ step) for i in range(8)])
    half = sum_four(sum_four(later(half, after), "x"), "y")
    other = swap_cores(half)
    first = jnp.where(c == 0, half, other)
    second = jnp.where(c == 0, other, half)
    return jnp.concatenate([first, second], axis=0)


def local(features, weight, cotangent, tile_values, tile_rows, tile_cols, tile_count, send_blocks):
    width = features.shape[1]
    node_total = features.shape[0] * lax.axis_size("col") * lax.axis_size(DOM)
    c = lax.axis_index("col")
    z_me = lax.axis_index("z")
    r_me = lax.axis_index(PLANE)
    where = jnp.stack([c, z_me, r_me]).astype(jnp.int32)

    ids_row = jnp.pad(send_blocks.astype(jnp.bfloat16), ((0, META - 1), (0, width - send_blocks.shape[1])))
    column = lax.all_gather(jnp.concatenate([features, ids_row], axis=0), "z", axis=0)
    packed = pack(tile_cols, tile_rows, tile_count, tile_values)
    sent = lax.all_to_all(packed, PLANE, 0, 0, tiled=True)
    cot_mine = lax.all_gather(later(cotangent, sent).reshape(4, BLK, width), PLANE, axis=0, tiled=True)

    meta = sent[:, 8 * BLK, :8].astype(jnp.int32).reshape(128)
    ids = column[:, 4 * BLK, :128].astype(jnp.int32).reshape(8, 16, 8)
    ids = lax.dynamic_index_in_dim(ids, z_me, 2, keepdims=False).reshape(128)

    operands = (where, meta, ids, tile_cols, tile_rows, tile_count, sent, column, tile_values)
    both = hidden_parts(*operands, swap_cores(hidden_parts(*operands)))
    parts = lax.all_to_all(both.reshape(16, 4 * BLK, width), PLANE, 0, 0, tiled=True)
    cot_mine = same_later(cot_mine, both)
    own, *away = grad_parts(*operands[:7], cot_mine, swap_cores(cot_mine), tile_values)
    by_partition = (16, 4 * BLK, width)
    term = weight_term(both.reshape(by_partition), cot_mine.reshape(by_partition), float(1.0 / node_total**0.5))
    arrived = [
        lax.ppermute(part, "z", [(z, (z + step) % 8) for z in range(8)])
        for step, part in sorted(enumerate(away, 1), key=lambda e: -min(e[0], 8 - e[0]))
    ]
    feature_grad = feature_from(own, arrived, weight)
    weight_grad = sum_everywhere(term, c, own)
    output_rows = output_from(parts, weight, feature_grad, weight_grad)
    return (output_rows, feature_grad, weight_grad)


def solution(mesh):
    grid = Mesh(mesh.devices.reshape(SIZES), ("y", "x", "z", "col"))
    every = ("y", "x", "z", "col")
    return jax.shard_map(
        local,
        mesh=grid,
        in_specs=(
            P(every, None),
            P(),
            P(every, None),
            P(every, None, None),
            P(every),
            P(every),
            P(every),
            P(every, None),
        ),
        out_specs=(P(every, None), P(every, None), P()),
        check_vma=False,
    )
```

```python
import functools

import jax
import jax.numpy as jnp
from jax import lax
from jax.experimental import pallas as pl
from jax.experimental.pallas import tpu as pltpu
from jax.sharding import Mesh
from jax.sharding import PartitionSpec as P

PLANE = ("y", "x")
DOM = ("y", "x", "z")
SIZES = (4, 4, 8, 2)
BLK = 128
META = 16


def pack_kernel(cols, rows, count, tiles, out):
    slots = out.shape[1] // BLK
    here = pl.ds(slots * BLK, META)
    lane = lax.broadcasted_iota(jnp.int32, (META, BLK), 1)
    line = lax.broadcasted_iota(jnp.int32, (META, BLK), 0)

    def clear(d, carry):
        out[d, here, :] = jnp.zeros((META, BLK), out.dtype)
        return carry

    lax.fori_loop(0, out.shape[0], clear, 0)

    def one(t, carry):
        @pl.when(cols[t] >= 4)
        def _():
            slot = jnp.maximum(cols[t] - 4, 0)
            d, z = lax.div(slot, slots), lax.rem(slot, slots)
            out[d, rows_at(z), :] = tiles[t]
            mark = jnp.where((lane == z) & (line == 0), rows[t] + 1, 0)
            out[d, here, :] = (out[d, here, :].astype(jnp.float32) + mark.astype(jnp.float32)).astype(out.dtype)

        return carry

    lax.fori_loop(0, count[0], one, 0)


def pack(cols, rows, count, tiles):
    groups, slots = 16, 8
    smem = pl.BlockSpec(memory_space=pltpu.SMEM)
    vmem = pl.BlockSpec(memory_space=pltpu.VMEM)
    return pl.pallas_call(
        pack_kernel,
        out_shape=jax.ShapeDtypeStruct((groups, slots * BLK + META, BLK), tiles.dtype),
        in_specs=[smem, smem, smem, vmem],
        out_specs=vmem,
        compiler_params=pltpu.CompilerParams(vmem_limit_bytes=12 * 2**20),
        cost_estimate=cost(3),
        name="pack_tiles",
    )(cols, rows, count, tiles)


def cost(us):
    return pl.CostEstimate(flops=us * 10**8, bytes_accessed=us * 3 * 10**6, transcendentals=0)


def rows_at(k):
    return pl.ds(pl.multiple_of(k * BLK, BLK), BLK)


def hidden_kernel(first, where, meta, ids, cols, rows, count, sent, tiles, *rest):
    feats, rest = rest[:8], rest[8:]
    out, total = rest[-2:]
    c, z_me, r_me = where[0], where[1], where[2]
    half = 1 - c if first else c

    def begin(i, carry):
        total[i] = jnp.zeros(total.shape[1:], total.dtype) if first else rest[0][i].astype(total.dtype)
        return carry

    lax.fori_loop(0, total.shape[0], begin, 0)

    def add(tile, block, r, row):
        at = r * 4 + lax.rem(row, 4)
        total[at] = total[at] + jnp.dot(tile, block, preferred_element_type=jnp.float32)

    for s in range(8):
        z = jnp.bitwise_and(z_me - s + 8, 7)

        def remote(r, carry, s=s, z=z):
            mark = meta[r * 8 + z]

            @pl.when((mark > 0) & (lax.div(mark - 1, 4) == half))
            def _():
                add(sent[r, rows_at(z), :], feats[s][rows_at(ids[s * 16 + r]), :], r, mark - 1)

            return carry

        lax.fori_loop(0, 16, remote, 0)

    def own(t, carry):
        @pl.when((cols[t] < 4) & (lax.div(rows[t], 4) == half))
        def _():
            add(tiles[t], feats[0][rows_at(jnp.minimum(cols[t], 3)), :], r_me, rows[t])

        return carry

    lax.fori_loop(0, count[0], own, 0)

    def cast(i, carry):
        out[i] = total[i].astype(out.dtype)
        return carry

    lax.fori_loop(0, total.shape[0], cast, 0)


def hidden_parts(where, meta, ids, cols, rows, count, sent, tiles, feats, *arrived):
    smem = pl.BlockSpec(memory_space=pltpu.SMEM)
    vmem = pl.BlockSpec(memory_space=pltpu.VMEM)
    width = feats[0].shape[1]
    return pl.pallas_call(
        functools.partial(hidden_kernel, not arrived),
        out_shape=jax.ShapeDtypeStruct((64, BLK, width), jnp.bfloat16),
        in_specs=[smem] * 6 + [vmem] * (2 + len(feats) + len(arrived)),
        out_specs=vmem,
        scratch_shapes=[pltpu.VMEM((64, BLK, width), jnp.float32)],
        compiler_params=pltpu.CompilerParams(vmem_limit_bytes=28 * 2**20),
        cost_estimate=cost(10),
        name="hidden_sums" if arrived else "hidden_for_other_core",
    )(where, meta, ids, cols, rows, count, sent, tiles, *feats, *arrived)


def add_grads(half, where, meta, ids, cols, rows, count, sent, grads, tiles, total):
    z_me, r_me = where[1], where[2]

    def add(at, tile, r, row):
        term = lax.dot_general(
            tile, grads[r * 4 + lax.rem(row, 4)], (((0,), (0,)), ((), ())),
            preferred_element_type=jnp.float32,
        )
        total[at] = total[at] + term

    def remote(i, carry):
        r, z = lax.div(i, 8), lax.rem(i, 8)
        row = meta[i] - 1

        @pl.when((meta[i] > 0) & (lax.div(row, 4) == half))
        def _():
            step, back = jnp.bitwise_and(z - z_me + 8, 7), jnp.bitwise_and(z_me - z + 8, 7)
            add(step * 4 + ids[back * 16 + r], sent[r, rows_at(z), :], r, row)

        return carry

    lax.fori_loop(0, 128, remote, 0)

    def own(t, carry):
        @pl.when((cols[t] < 4) & (lax.div(rows[t], 4) == half))
        def _():
            add(jnp.minimum(cols[t], 3), tiles[t], r_me, rows[t])

        return carry

    lax.fori_loop(0, count[0], own, 0)


def grad_kernel(where, meta, ids, cols, rows, count, sent, mine, peer, tiles, *outs):
    total = outs[-1]

    def begin(i, carry):
        total[i] = jnp.zeros(total.shape[1:], total.dtype)
        return carry

    lax.fori_loop(0, total.shape[0], begin, 0)
    add_grads(where[0], where, meta, ids, cols, rows, count, sent, mine, tiles, total)
    add_grads(1 - where[0], where, meta, ids, cols, rows, count, sent, peer, tiles, total)
    for k in range(4):
        outs[0][rows_at(k), :] = total[k]
    for step in range(1, 8):
        for k in range(4):
            outs[step][rows_at(k), :] = total[step * 4 + k].astype(outs[step].dtype)


def grad_parts(where, meta, ids, cols, rows, count, sent, mine, peer, tiles):
    smem = pl.BlockSpec(memory_space=pltpu.SMEM)
    vmem = pl.BlockSpec(memory_space=pltpu.VMEM)
    width = mine.shape[2]
    return pl.pallas_call(
        grad_kernel,
        out_shape=[jax.ShapeDtypeStruct((4 * BLK, width), jnp.float32)]
        + [jax.ShapeDtypeStruct((4 * BLK, width), jnp.bfloat16)] * 7,
        in_specs=[smem] * 6 + [vmem] * 4,
        out_specs=[vmem] * 8,
        scratch_shapes=[pltpu.VMEM((32, BLK, width), jnp.float32)],
        compiler_params=pltpu.CompilerParams(vmem_limit_bytes=28 * 2**20),
        cost_estimate=cost(8),
        name="grad_sums",
    )(where, meta, ids, cols, rows, count, sent, mine, peer, tiles)


def term_kernel(scale, parts, cots, term):
    term[...] = jnp.zeros(term.shape, term.dtype)

    def product(i, carry):
        term[...] += lax.dot_general(
            parts[i], cots[i], (((0,), (0,)), ((), ())), preferred_element_type=jnp.float32
        )
        return carry

    lax.fori_loop(0, parts.shape[0], product, 0)
    term[...] = term[...] * scale


def weight_term(parts, cots, scale):
    vmem = pl.BlockSpec(memory_space=pltpu.VMEM)
    width = parts.shape[2]
    return pl.pallas_call(
        functools.partial(term_kernel, scale),
        out_shape=jax.ShapeDtypeStruct((width, width), jnp.float32),
        in_specs=[vmem] * 2,
        out_specs=vmem,
        compiler_params=pltpu.CompilerParams(vmem_limit_bytes=12 * 2**20),
        cost_estimate=cost(4),
        name="weight_term",
    )(parts, cots)


def output_kernel(parts, weight, *rest):
    output = rest[-1]
    total = parts[0].astype(jnp.float32)
    for i in range(1, parts.shape[0]):
        total = total + parts[i].astype(jnp.float32)
    hidden = total.astype(jnp.bfloat16)
    output[...] = jnp.dot(hidden, weight[...], preferred_element_type=jnp.float32).astype(output.dtype)


def output_from(parts, weight, *after):
    vmem = pl.BlockSpec(memory_space=pltpu.VMEM)
    return pl.pallas_call(
        output_kernel,
        out_shape=jax.ShapeDtypeStruct(parts.shape[1:], jnp.bfloat16),
        in_specs=[vmem] * 2 + [pl.BlockSpec(memory_space=pl.ANY)] * len(after),
        out_specs=vmem,
        compiler_params=pltpu.CompilerParams(vmem_limit_bytes=16 * 2**20),
        cost_estimate=cost(4),
        name="output_rows",
    )(parts, weight, *after)


def feature_kernel(own, *rest):
    weight, out = rest[-2:]
    total = own[...]
    for part in rest[:-2]:
        total = total + part[...].astype(jnp.float32)
    high = total.astype(jnp.bfloat16)
    low = (total - high.astype(jnp.float32)).astype(jnp.bfloat16)
    dims = (((1,), (1,)), ((), ()))
    grad = lax.dot_general(high, weight[...], dims, preferred_element_type=jnp.float32)
    grad = grad + lax.dot_general(low, weight[...], dims, preferred_element_type=jnp.float32)
    out[...] = grad.astype(out.dtype)


def feature_from(own, parts, weight):
    vmem = pl.BlockSpec(memory_space=pltpu.VMEM)
    return pl.pallas_call(
        feature_kernel,
        out_shape=jax.ShapeDtypeStruct(own.shape, jnp.bfloat16),
        in_specs=[vmem] * (2 + len(parts)),
        out_specs=vmem,
        compiler_params=pltpu.CompilerParams(vmem_limit_bytes=16 * 2**20),
        cost_estimate=cost(4),
        name="feature_gradient",
    )(own, *parts, weight)


def join_kernel(*refs):
    out, at = refs[-1], 0
    for ref in refs[:-2]:
        out[pl.ds(at, ref.shape[0]), :] = ref[...]
        at += ref.shape[0]


def join_later(arrays, after):
    vmem = pl.BlockSpec(memory_space=pltpu.VMEM)
    length = sum(a.shape[0] for a in arrays)
    return pl.pallas_call(
        join_kernel,
        out_shape=jax.ShapeDtypeStruct((length, arrays[0].shape[1]), arrays[0].dtype),
        in_specs=[vmem] * len(arrays) + [pl.BlockSpec(memory_space=pl.ANY)],
        out_specs=vmem,
        compiler_params=pltpu.CompilerParams(vmem_limit_bytes=12 * 2**20),
        cost_estimate=cost(1),
        name="in_order",
    )(*arrays, after)


def same_later_kernel(*refs):
    del refs


def same_later(arrays, after):
    hbm = pl.BlockSpec(memory_space=pl.ANY)
    return pl.pallas_call(
        same_later_kernel,
        out_shape=[jax.ShapeDtypeStruct(a.shape, a.dtype) for a in arrays],
        in_specs=[hbm] * (len(arrays) + 1),
        out_specs=[hbm] * len(arrays),
        input_output_aliases={i: i for i in range(len(arrays))},
        cost_estimate=cost(1),
        name="in_order_in_place",
    )(*arrays, after)


def swap_cores(a):
    return lax.ppermute(a, "col", [(0, 1), (1, 0)])


def steps_along(a, axis, size):
    return [a] + [lax.ppermute(a, axis, [(i, (i + s) % size) for i in range(size)]) for s in range(1, size)]


def mark(*arrays):
    return jnp.concatenate([a.reshape(-1, a.shape[-1])[:META].astype(jnp.bfloat16) for a in arrays], axis=0)


def sum_four(a, axis):
    me = lax.axis_index(axis)
    from_step = steps_along(a, axis, 4)
    total = None
    for source in range(4):
        step = jnp.bitwise_and(me - source + 4, 3)
        low = jnp.where(step == 0, from_step[0], from_step[1])
        high = jnp.where(step == 2, from_step[2], from_step[3])
        part = jnp.where(step < 2, low, high)
        total = part if total is None else total + part
    return total


def sum_everywhere(term, c, after):
    halves = term.reshape(2, 128, term.shape[1])
    keep = lax.dynamic_index_in_dim(halves, c, 0, keepdims=False)
    give = lax.dynamic_index_in_dim(halves, 1 - c, 0, keepdims=False)
    half = join_later([keep + swap_cores(give)], after)
    half = sum_four(sum_four(half, "x"), "y")
    for step in (1, 2, 4):
        half = half + lax.ppermute(half, "z", [(i, i ^ step) for i in range(8)])
    other = swap_cores(half)
    first = jnp.where(c == 0, half, other)
    second = jnp.where(c == 0, other, half)
    return jnp.concatenate([first, second], axis=0)


def local(features, weight, cotangent, tile_values, tile_rows, tile_cols, tile_count, send_blocks):
    width = features.shape[1]
    node_total = features.shape[0] * lax.axis_size("col") * lax.axis_size(DOM)
    c = lax.axis_index("col")
    z_me = lax.axis_index("z")
    r_me = lax.axis_index(PLANE)
    where = jnp.stack([c, z_me, r_me, lax.axis_index("y"), lax.axis_index("x")]).astype(jnp.int32)

    ids_row = jnp.pad(send_blocks.astype(jnp.bfloat16), ((0, META - 1), (0, width - send_blocks.shape[1])))
    feats = steps_along(jnp.concatenate([features, ids_row], axis=0), "z", 8)
    cot_mine = lax.all_gather(cotangent.reshape(4, BLK, width), PLANE, axis=0, tiled=True)
    packed = pack(tile_cols, tile_rows, tile_count, tile_values)
    sent = lax.all_to_all(packed, PLANE, 0, 0, tiled=True)

    meta = sent[:, 8 * BLK, :8].astype(jnp.int32).reshape(128)
    ids = jnp.stack([f[4 * BLK, :128] for f in feats]).astype(jnp.int32).reshape(8, 16, 8)
    ids = lax.dynamic_index_in_dim(ids, z_me, 2, keepdims=False).reshape(128)

    operands = (where, meta, ids, tile_cols, tile_rows, tile_count, sent)
    for_peer = swap_cores(hidden_parts(*operands, tile_values, feats))
    both = hidden_parts(*operands, tile_values, feats, for_peer)
    parts = lax.all_to_all(both.reshape(16, 4 * BLK, width), PLANE, 0, 0, tiled=True)
    [cot_mine] = same_later([cot_mine], mark(both))
    own, *away = grad_parts(*operands, cot_mine, swap_cores(cot_mine), tile_values)
    by_partition = (16, 4 * BLK, width)
    term = weight_term(both.reshape(by_partition), cot_mine.reshape(by_partition), float(1.0 / node_total**0.5))
    term = join_later([term], mark(own))
    arrived = [
        lax.ppermute(part, "z", [(z, (z + step) % 8) for z in range(8)])
        for step, part in sorted(enumerate(away, 1), key=lambda e: -min(e[0], 8 - e[0]))
    ]
    feature_grad = feature_from(own, arrived, weight)
    weight_grad = sum_everywhere(term, c, mark(*arrived[:5]))
    output_rows = output_from(parts, weight)
    return (output_rows, feature_grad, weight_grad)


def solution(mesh):
    grid = Mesh(mesh.devices.reshape(SIZES), ("y", "x", "z", "col"))
    every = ("y", "x", "z", "col")
    return jax.shard_map(
        local,
        mesh=grid,
        in_specs=(
            P(every, None),
            P(),
            P(every, None),
            P(every, None, None),
            P(every),
            P(every),
            P(every),
            P(every, None),
        ),
        out_specs=(P(every, None), P(every, None), P()),
        check_vma=False,
    )
```

```python
import functools

import jax
import jax.numpy as jnp
from jax import lax
from jax.experimental import pallas as pl
from jax.experimental.pallas import tpu as pltpu
from jax.sharding import Mesh
from jax.sharding import PartitionSpec as P

PLANE = ("y", "x")
DOM = ("y", "x", "z")
SIZES = (4, 4, 8, 2)
BLK = 128
META = 16


def pack_kernel(cols, rows, count, tiles, out):
    slots = out.shape[1] // BLK
    here = pl.ds(slots * BLK, META)
    lane = lax.broadcasted_iota(jnp.int32, (META, BLK), 1)
    line = lax.broadcasted_iota(jnp.int32, (META, BLK), 0)

    def clear(d, carry):
        out[d, here, :] = jnp.zeros((META, BLK), out.dtype)
        return carry

    lax.fori_loop(0, out.shape[0], clear, 0)

    def one(t, carry):
        @pl.when(cols[t] >= 4)
        def _():
            slot = jnp.maximum(cols[t] - 4, 0)
            d, z = lax.div(slot, slots), lax.rem(slot, slots)
            out[d, rows_at(z), :] = tiles[t]
            mark = jnp.where((lane == z) & (line == 0), rows[t] + 1, 0)
            out[d, here, :] = (out[d, here, :].astype(jnp.float32) + mark.astype(jnp.float32)).astype(out.dtype)

        return carry

    lax.fori_loop(0, count[0], one, 0)


def pack(cols, rows, count, tiles):
    groups, slots = 16, 8
    smem = pl.BlockSpec(memory_space=pltpu.SMEM)
    vmem = pl.BlockSpec(memory_space=pltpu.VMEM)
    return pl.pallas_call(
        pack_kernel,
        out_shape=jax.ShapeDtypeStruct((groups, slots * BLK + META, BLK), tiles.dtype),
        in_specs=[smem, smem, smem, vmem],
        out_specs=vmem,
        compiler_params=pltpu.CompilerParams(vmem_limit_bytes=12 * 2**20),
        cost_estimate=cost(3),
        name="pack_tiles",
    )(cols, rows, count, tiles)


def cost(us):
    return pl.CostEstimate(flops=us * 10**8, bytes_accessed=us * 3 * 10**6, transcendentals=0)


def rows_at(k):
    return pl.ds(pl.multiple_of(k * BLK, BLK), BLK)


def hidden_kernel(first, where, meta, ids, cols, rows, count, sent, tiles, *rest):
    feats, rest = rest[:8], rest[8:]
    out, total = rest[-2:]
    c, z_me, r_me = where[0], where[1], where[2]
    half = 1 - c if first else c

    def begin(i, carry):
        total[i] = jnp.zeros(total.shape[1:], total.dtype) if first else rest[0][i].astype(total.dtype)
        return carry

    lax.fori_loop(0, total.shape[0], begin, 0)

    def add(tile, block, r, row):
        at = r * 4 + lax.rem(row, 4)
        total[at] = total[at] + jnp.dot(tile, block, preferred_element_type=jnp.float32)

    for s in range(8):
        z = jnp.bitwise_and(z_me - s + 8, 7)

        def remote(r, carry, s=s, z=z):
            mark = meta[r * 8 + z]

            @pl.when((mark > 0) & (lax.div(mark - 1, 4) == half))
            def _():
                add(sent[r, rows_at(z), :], feats[s][rows_at(ids[s * 16 + r]), :], r, mark - 1)

            return carry

        lax.fori_loop(0, 16, remote, 0)

    def own(t, carry):
        @pl.when((cols[t] < 4) & (lax.div(rows[t], 4) == half))
        def _():
            add(tiles[t], feats[0][rows_at(jnp.minimum(cols[t], 3)), :], r_me, rows[t])

        return carry

    lax.fori_loop(0, count[0], own, 0)

    def cast(i, carry):
        out[i] = total[i].astype(out.dtype)
        return carry

    lax.fori_loop(0, total.shape[0], cast, 0)


def hidden_parts(where, meta, ids, cols, rows, count, sent, tiles, feats, *arrived):
    smem = pl.BlockSpec(memory_space=pltpu.SMEM)
    vmem = pl.BlockSpec(memory_space=pltpu.VMEM)
    width = feats[0].shape[1]
    return pl.pallas_call(
        functools.partial(hidden_kernel, not arrived),
        out_shape=jax.ShapeDtypeStruct((64, BLK, width), jnp.bfloat16),
        in_specs=[smem] * 6 + [vmem] * (2 + len(feats) + len(arrived)),
        out_specs=vmem,
        scratch_shapes=[pltpu.VMEM((64, BLK, width), jnp.float32)],
        compiler_params=pltpu.CompilerParams(vmem_limit_bytes=28 * 2**20),
        cost_estimate=cost(10),
        name="hidden_sums" if arrived else "hidden_for_other_core",
    )(where, meta, ids, cols, rows, count, sent, tiles, *feats, *arrived)


def add_grads(where, meta, ids, cols, rows, count, sent, mine, peer, tiles, total):
    c, z_me, r_me = where[0], where[1], where[2]

    def add(at, tile, r, row):
        def go(cots):
            term = lax.dot_general(
                tile, cots[r * 4 + lax.rem(row, 4)], (((0,), (0,)), ((), ())), preferred_element_type=jnp.float32
            )
            total[at] = total[at] + term

        @pl.when(lax.div(row, 4) == c)
        def _():
            go(mine)

        @pl.when(lax.div(row, 4) != c)
        def _():
            go(peer)

    def remote(i, carry):
        r, z = lax.div(i, 8), lax.rem(i, 8)

        @pl.when(meta[i] > 0)
        def _():
            step, back = jnp.bitwise_and(z - z_me + 8, 7), jnp.bitwise_and(z_me - z + 8, 7)
            add(step * 4 + ids[back * 16 + r], sent[r, rows_at(z), :], r, meta[i] - 1)

        return carry

    lax.fori_loop(0, 128, remote, 0)

    def own(t, carry):
        @pl.when(cols[t] < 4)
        def _():
            add(jnp.minimum(cols[t], 3), tiles[t], r_me, rows[t])

        return carry

    lax.fori_loop(0, count[0], own, 0)


def grad_kernel(where, meta, ids, cols, rows, count, sent, mine, peer, tiles, *outs):
    total = outs[-1]

    def begin(i, carry):
        total[i] = jnp.zeros(total.shape[1:], total.dtype)
        return carry

    lax.fori_loop(0, total.shape[0], begin, 0)
    add_grads(where, meta, ids, cols, rows, count, sent, mine, peer, tiles, total)
    for k in range(4):
        outs[0][rows_at(k), :] = total[k]
    for step in range(1, 8):
        for k in range(4):
            outs[step][rows_at(k), :] = total[step * 4 + k].astype(outs[step].dtype)


def grad_parts(where, meta, ids, cols, rows, count, sent, mine, peer, tiles):
    smem = pl.BlockSpec(memory_space=pltpu.SMEM)
    vmem = pl.BlockSpec(memory_space=pltpu.VMEM)
    width = mine.shape[2]
    return pl.pallas_call(
        grad_kernel,
        out_shape=[jax.ShapeDtypeStruct((4 * BLK, width), jnp.float32)]
        + [jax.ShapeDtypeStruct((4 * BLK, width), jnp.bfloat16)] * 7,
        in_specs=[smem] * 6 + [vmem] * 4,
        out_specs=[vmem] * 8,
        scratch_shapes=[pltpu.VMEM((32, BLK, width), jnp.float32)],
        compiler_params=pltpu.CompilerParams(vmem_limit_bytes=28 * 2**20),
        cost_estimate=cost(8),
        name="grad_sums",
    )(where, meta, ids, cols, rows, count, sent, mine, peer, tiles)


def term_kernel(scale, parts, cots, after, term):
    del after
    term[...] = jnp.zeros(term.shape, term.dtype)

    def product(i, carry):
        term[...] += lax.dot_general(
            parts[i], cots[i], (((0,), (0,)), ((), ())), preferred_element_type=jnp.float32
        )
        return carry

    lax.fori_loop(0, parts.shape[0], product, 0)
    term[...] = term[...] * scale


def weight_term(parts, cots, after, scale):
    vmem = pl.BlockSpec(memory_space=pltpu.VMEM)
    width = parts.shape[2]
    return pl.pallas_call(
        functools.partial(term_kernel, scale),
        out_shape=jax.ShapeDtypeStruct((width, width), jnp.float32),
        in_specs=[vmem] * 2 + [pl.BlockSpec(memory_space=pl.ANY)],
        out_specs=vmem,
        compiler_params=pltpu.CompilerParams(vmem_limit_bytes=12 * 2**20),
        cost_estimate=cost(4),
        name="weight_term",
    )(parts, cots, after)


def output_kernel(parts, weight, *rest):
    output = rest[-1]
    total = parts[0].astype(jnp.float32)
    for i in range(1, parts.shape[0]):
        total = total + parts[i].astype(jnp.float32)
    hidden = total.astype(jnp.bfloat16)
    output[...] = jnp.dot(hidden, weight[...], preferred_element_type=jnp.float32).astype(output.dtype)


def output_from(parts, weight, *after):
    vmem = pl.BlockSpec(memory_space=pltpu.VMEM)
    return pl.pallas_call(
        output_kernel,
        out_shape=jax.ShapeDtypeStruct(parts.shape[1:], jnp.bfloat16),
        in_specs=[vmem] * 2 + [pl.BlockSpec(memory_space=pl.ANY)] * len(after),
        out_specs=vmem,
        compiler_params=pltpu.CompilerParams(vmem_limit_bytes=16 * 2**20),
        cost_estimate=cost(4),
        name="output_rows",
    )(parts, weight, *after)


def feature_kernel(own, *rest):
    weight, out = rest[-2:]
    total = own[...]
    for part in rest[:-2]:
        total = total + part[...].astype(jnp.float32)
    high = total.astype(jnp.bfloat16)
    low = (total - high.astype(jnp.float32)).astype(jnp.bfloat16)
    dims = (((1,), (1,)), ((), ()))
    grad = lax.dot_general(high, weight[...], dims, preferred_element_type=jnp.float32)
    grad = grad + lax.dot_general(low, weight[...], dims, preferred_element_type=jnp.float32)
    out[...] = grad.astype(out.dtype)


def feature_from(own, parts, weight):
    vmem = pl.BlockSpec(memory_space=pltpu.VMEM)
    return pl.pallas_call(
        feature_kernel,
        out_shape=jax.ShapeDtypeStruct(own.shape, jnp.bfloat16),
        in_specs=[vmem] * (2 + len(parts)),
        out_specs=vmem,
        compiler_params=pltpu.CompilerParams(vmem_limit_bytes=16 * 2**20),
        cost_estimate=cost(4),
        name="feature_gradient",
    )(own, *parts, weight)


def join_kernel(*refs):
    out, at = refs[-1], 0
    for ref in refs[:-2]:
        out[pl.ds(at, ref.shape[0]), :] = ref[...]
        at += ref.shape[0]


def join_later(arrays, after):
    vmem = pl.BlockSpec(memory_space=pltpu.VMEM)
    length = sum(a.shape[0] for a in arrays)
    return pl.pallas_call(
        join_kernel,
        out_shape=jax.ShapeDtypeStruct((length, arrays[0].shape[1]), arrays[0].dtype),
        in_specs=[vmem] * len(arrays) + [pl.BlockSpec(memory_space=pl.ANY)],
        out_specs=vmem,
        compiler_params=pltpu.CompilerParams(vmem_limit_bytes=12 * 2**20),
        cost_estimate=cost(1),
        name="in_order",
    )(*arrays, after)


def same_later_kernel(*refs):
    del refs


def same_later(arrays, after):
    hbm = pl.BlockSpec(memory_space=pl.ANY)
    return pl.pallas_call(
        same_later_kernel,
        out_shape=[jax.ShapeDtypeStruct(a.shape, a.dtype) for a in arrays],
        in_specs=[hbm] * (len(arrays) + 1),
        out_specs=[hbm] * len(arrays),
        input_output_aliases={i: i for i in range(len(arrays))},
        cost_estimate=cost(1),
        name="in_order_in_place",
    )(*arrays, after)


def swap_cores(a):
    return lax.ppermute(a, "col", [(0, 1), (1, 0)])


def steps_along(a, axis, size):
    return [a] + [lax.ppermute(a, axis, [(i, (i + s) % size) for i in range(size)]) for s in range(1, size)]


def mark(*arrays):
    return jnp.concatenate([a.reshape(-1, a.shape[-1])[:8].astype(jnp.bfloat16) for a in arrays], axis=0)


def sum_everywhere(term, c, after, before_last):
    n = term.shape[1]
    halves = term.reshape(2, 128, n)
    keep = lax.dynamic_index_in_dim(halves, c, 0, keepdims=False)
    give = lax.dynamic_index_in_dim(halves, 1 - c, 0, keepdims=False)
    half = join_later([keep + swap_cores(give)], after)
    rows = jnp.sum(lax.all_to_all(half.reshape(16, 8, n), PLANE, 0, 0, tiled=True), axis=0)
    for step in (1, 2, 4):
        rows = rows + lax.ppermute(rows, "z", [(i, i ^ step) for i in range(8)])
    rows = join_later([rows], before_last)
    half = lax.all_to_all(jnp.broadcast_to(rows[None], (16, 8, n)), PLANE, 0, 0, tiled=True).reshape(128, n)
    other = swap_cores(half)
    first = jnp.where(c == 0, half, other)
    second = jnp.where(c == 0, other, half)
    return jnp.concatenate([first, second], axis=0)


def local(features, weight, cotangent, tile_values, tile_rows, tile_cols, tile_count, send_blocks):
    width = features.shape[1]
    node_total = features.shape[0] * lax.axis_size("col") * lax.axis_size(DOM)
    c = lax.axis_index("col")
    z_me = lax.axis_index("z")
    r_me = lax.axis_index(PLANE)
    where = jnp.stack([c, z_me, r_me, lax.axis_index("y"), lax.axis_index("x")]).astype(jnp.int32)

    ids_row = jnp.pad(send_blocks.astype(jnp.bfloat16), ((0, META - 1), (0, width - send_blocks.shape[1])))
    feats = steps_along(jnp.concatenate([features, ids_row], axis=0), "z", 8)
    cot_mine = lax.all_gather(cotangent.reshape(4, BLK, width), PLANE, axis=0, tiled=True)
    packed = pack(tile_cols, tile_rows, tile_count, tile_values)
    sent = lax.all_to_all(packed, PLANE, 0, 0, tiled=True)

    meta = sent[:, 8 * BLK, :8].astype(jnp.int32).reshape(128)
    ids = jnp.stack([f[4 * BLK, :128] for f in feats]).astype(jnp.int32).reshape(8, 16, 8)
    ids = lax.dynamic_index_in_dim(ids, z_me, 2, keepdims=False).reshape(128)

    operands = (where, meta, ids, tile_cols, tile_rows, tile_count, sent)
    for_peer = swap_cores(hidden_parts(*operands, tile_values, feats))
    both = hidden_parts(*operands, tile_values, feats, for_peer)
    parts = lax.all_to_all(both.reshape(16, 4 * BLK, width), PLANE, 0, 0, tiled=True)
    [cot_mine] = same_later([cot_mine], mark(both))
    own, *away = grad_parts(*operands, cot_mine, swap_cores(cot_mine), tile_values)
    by_partition = (16, 4 * BLK, width)
    scale = float(1.0 / node_total**0.5)
    term = weight_term(both.reshape(by_partition), cot_mine.reshape(by_partition), mark(own), scale)
    arrived = [
        lax.ppermute(part, "z", [(z, (z + step) % 8) for z in range(8)])
        for step, part in sorted(enumerate(away, 1), key=lambda e: -min(e[0], 8 - e[0]))
    ]
    feature_grad = feature_from(own, arrived, weight)
    output_rows = output_from(parts, weight)
    gate = join_later([mark(*arrived[:5])], parts)
    weight_grad = sum_everywhere(term, c, gate, mark(output_rows))
    return (output_rows, feature_grad, weight_grad)


def solution(mesh):
    grid = Mesh(mesh.devices.reshape(SIZES), ("y", "x", "z", "col"))
    every = ("y", "x", "z", "col")
    return jax.shard_map(
        local,
        mesh=grid,
        in_specs=(
            P(every, None),
            P(),
            P(every, None),
            P(every, None, None),
            P(every),
            P(every),
            P(every),
            P(every, None),
        ),
        out_specs=(P(every, None), P(every, None), P()),
        check_vma=False,
    )
```

```python
import functools

import jax
import jax.numpy as jnp
from jax import lax
from jax.experimental import pallas as pl
from jax.experimental.pallas import tpu as pltpu
from jax.sharding import Mesh
from jax.sharding import PartitionSpec as P

PLANE = ("y", "x")
DOM = ("y", "x", "z")
SIZES = (4, 4, 8, 2)
BLK = 128
META = 16


def pack_kernel(cols, rows, count, tiles, out):
    slots = out.shape[1] // BLK
    here = pl.ds(slots * BLK, META)
    lane = lax.broadcasted_iota(jnp.int32, (META, BLK), 1)
    line = lax.broadcasted_iota(jnp.int32, (META, BLK), 0)

    def clear(d, carry):
        out[d, here, :] = jnp.zeros((META, BLK), out.dtype)
        return carry

    lax.fori_loop(0, out.shape[0], clear, 0)

    def one(t, carry):
        @pl.when(cols[t] >= 4)
        def _():
            slot = jnp.maximum(cols[t] - 4, 0)
            d, z = lax.div(slot, slots), lax.rem(slot, slots)
            out[d, rows_at(z), :] = tiles[t]
            mark = jnp.where((lane == z) & (line == 0), rows[t] + 1, 0)
            out[d, here, :] = (out[d, here, :].astype(jnp.float32) + mark.astype(jnp.float32)).astype(out.dtype)

        return carry

    lax.fori_loop(0, count[0], one, 0)


def pack(cols, rows, count, tiles):
    groups, slots = 16, 8
    smem = pl.BlockSpec(memory_space=pltpu.SMEM)
    vmem = pl.BlockSpec(memory_space=pltpu.VMEM)
    return pl.pallas_call(
        pack_kernel,
        out_shape=jax.ShapeDtypeStruct((groups, slots * BLK + META, BLK), tiles.dtype),
        in_specs=[smem, smem, smem, vmem],
        out_specs=vmem,
        compiler_params=pltpu.CompilerParams(vmem_limit_bytes=12 * 2**20),
        cost_estimate=cost(3),
        name="pack_tiles",
    )(cols, rows, count, tiles)


def cost(us):
    return pl.CostEstimate(flops=us * 10**8, bytes_accessed=us * 3 * 10**6, transcendentals=0)


def rows_at(k):
    return pl.ds(pl.multiple_of(k * BLK, BLK), BLK)


def hidden_kernel(first, where, meta, ids, cols, rows, count, sent, tiles, *rest):
    feats, rest = rest[:8], rest[8:]
    out, total = rest[-2:]
    c, z_me, r_me = where[0], where[1], where[2]
    half = 1 - c if first else c

    def begin(i, carry):
        total[i] = jnp.zeros(total.shape[1:], total.dtype) if first else rest[0][i].astype(total.dtype)
        return carry

    lax.fori_loop(0, total.shape[0], begin, 0)

    def add(tile, block, r, row):
        at = r * 4 + lax.rem(row, 4)
        total[at] = total[at] + jnp.dot(tile, block, preferred_element_type=jnp.float32)

    for s in range(8):
        z = jnp.bitwise_and(z_me - s + 8, 7)

        def remote(r, carry, s=s, z=z):
            mark = meta[r * 8 + z]

            @pl.when((mark > 0) & (lax.div(mark - 1, 4) == half))
            def _():
                add(sent[r, rows_at(z), :], feats[s][rows_at(ids[s * 16 + r]), :], r, mark - 1)

            return carry

        lax.fori_loop(0, 16, remote, 0, unroll=2)

    def own(t, carry):
        @pl.when((cols[t] < 4) & (lax.div(rows[t], 4) == half))
        def _():
            add(tiles[t], feats[0][rows_at(jnp.minimum(cols[t], 3)), :], r_me, rows[t])

        return carry

    lax.fori_loop(0, count[0], own, 0)

    def cast(i, carry):
        out[i] = total[i].astype(out.dtype)
        return carry

    lax.fori_loop(0, total.shape[0], cast, 0)


def hidden_parts(where, meta, ids, cols, rows, count, sent, tiles, feats, *arrived):
    smem = pl.BlockSpec(memory_space=pltpu.SMEM)
    vmem = pl.BlockSpec(memory_space=pltpu.VMEM)
    width = feats[0].shape[1]
    return pl.pallas_call(
        functools.partial(hidden_kernel, not arrived),
        out_shape=jax.ShapeDtypeStruct((64, BLK, width), jnp.bfloat16),
        in_specs=[smem] * 6 + [vmem] * (2 + len(feats) + len(arrived)),
        out_specs=vmem,
        scratch_shapes=[pltpu.VMEM((64, BLK, width), jnp.float32)],
        compiler_params=pltpu.CompilerParams(vmem_limit_bytes=28 * 2**20),
        cost_estimate=cost(10),
        name="hidden_sums" if arrived else "hidden_for_other_core",
    )(where, meta, ids, cols, rows, count, sent, tiles, *feats, *arrived)


def add_grads(where, meta, ids, cols, rows, count, sent, mine, peer, tiles, total):
    c, z_me, r_me = where[0], where[1], where[2]

    def add(at, tile, r, row):
        def go(cots):
            term = lax.dot_general(
                tile, cots[r * 4 + lax.rem(row, 4)], (((0,), (0,)), ((), ())), preferred_element_type=jnp.float32
            )
            total[at] = total[at] + term

        @pl.when(lax.div(row, 4) == c)
        def _():
            go(mine)

        @pl.when(lax.div(row, 4) != c)
        def _():
            go(peer)

    def remote(i, carry):
        r, z = lax.div(i, 8), lax.rem(i, 8)

        @pl.when(meta[i] > 0)
        def _():
            step, back = jnp.bitwise_and(z - z_me + 8, 7), jnp.bitwise_and(z_me - z + 8, 7)
            add(step * 4 + ids[back * 16 + r], sent[r, rows_at(z), :], r, meta[i] - 1)

        return carry

    lax.fori_loop(0, 128, remote, 0, unroll=4)

    def own(t, carry):
        @pl.when(cols[t] < 4)
        def _():
            add(jnp.minimum(cols[t], 3), tiles[t], r_me, rows[t])

        return carry

    lax.fori_loop(0, count[0], own, 0)


def grad_kernel(where, meta, ids, cols, rows, count, sent, mine, peer, tiles, *outs):
    total = outs[-1]

    def begin(i, carry):
        total[i] = jnp.zeros(total.shape[1:], total.dtype)
        return carry

    lax.fori_loop(0, total.shape[0], begin, 0)
    add_grads(where, meta, ids, cols, rows, count, sent, mine, peer, tiles, total)
    for k in range(4):
        outs[0][rows_at(k), :] = total[k]
    for step in range(1, 8):
        for k in range(4):
            outs[step][rows_at(k), :] = total[step * 4 + k].astype(outs[step].dtype)


def grad_parts(where, meta, ids, cols, rows, count, sent, mine, peer, tiles):
    smem = pl.BlockSpec(memory_space=pltpu.SMEM)
    vmem = pl.BlockSpec(memory_space=pltpu.VMEM)
    width = mine.shape[2]
    return pl.pallas_call(
        grad_kernel,
        out_shape=[jax.ShapeDtypeStruct((4 * BLK, width), jnp.float32)]
        + [jax.ShapeDtypeStruct((4 * BLK, width), jnp.bfloat16)] * 7,
        in_specs=[smem] * 6 + [vmem] * 4,
        out_specs=[vmem] * 8,
        scratch_shapes=[pltpu.VMEM((32, BLK, width), jnp.float32)],
        compiler_params=pltpu.CompilerParams(vmem_limit_bytes=28 * 2**20),
        cost_estimate=cost(8),
        name="grad_sums",
    )(where, meta, ids, cols, rows, count, sent, mine, peer, tiles)


def term_kernel(scale, parts, cots, after, term):
    del after
    term[...] = jnp.zeros(term.shape, term.dtype)

    def product(i, carry):
        term[...] += lax.dot_general(
            parts[i], cots[i], (((0,), (0,)), ((), ())), preferred_element_type=jnp.float32
        )
        return carry

    lax.fori_loop(0, parts.shape[0], product, 0)
    term[...] = term[...] * scale


def weight_term(parts, cots, after, scale):
    vmem = pl.BlockSpec(memory_space=pltpu.VMEM)
    width = parts.shape[2]
    return pl.pallas_call(
        functools.partial(term_kernel, scale),
        out_shape=jax.ShapeDtypeStruct((width, width), jnp.float32),
        in_specs=[vmem] * 2 + [pl.BlockSpec(memory_space=pl.ANY)],
        out_specs=vmem,
        compiler_params=pltpu.CompilerParams(vmem_limit_bytes=12 * 2**20),
        cost_estimate=cost(4),
        name="weight_term",
    )(parts, cots, after)


def output_kernel(parts, weight, *rest):
    output = rest[-1]
    total = parts[0].astype(jnp.float32)
    for i in range(1, parts.shape[0]):
        total = total + parts[i].astype(jnp.float32)
    hidden = total.astype(jnp.bfloat16)
    output[...] = jnp.dot(hidden, weight[...], preferred_element_type=jnp.float32).astype(output.dtype)


def output_from(parts, weight, *after):
    vmem = pl.BlockSpec(memory_space=pltpu.VMEM)
    return pl.pallas_call(
        output_kernel,
        out_shape=jax.ShapeDtypeStruct(parts.shape[1:], jnp.bfloat16),
        in_specs=[vmem] * 2 + [pl.BlockSpec(memory_space=pl.ANY)] * len(after),
        out_specs=vmem,
        compiler_params=pltpu.CompilerParams(vmem_limit_bytes=16 * 2**20),
        cost_estimate=cost(4),
        name="output_rows",
    )(parts, weight, *after)


def feature_kernel(own, *rest):
    weight, out = rest[-2:]
    total = own[...]
    for part in rest[:-2]:
        total = total + part[...].astype(jnp.float32)
    high = total.astype(jnp.bfloat16)
    low = (total - high.astype(jnp.float32)).astype(jnp.bfloat16)
    dims = (((1,), (1,)), ((), ()))
    grad = lax.dot_general(high, weight[...], dims, preferred_element_type=jnp.float32)
    grad = grad + lax.dot_general(low, weight[...], dims, preferred_element_type=jnp.float32)
    out[...] = grad.astype(out.dtype)


def feature_from(own, parts, weight):
    vmem = pl.BlockSpec(memory_space=pltpu.VMEM)
    return pl.pallas_call(
        feature_kernel,
        out_shape=jax.ShapeDtypeStruct(own.shape, jnp.bfloat16),
        in_specs=[vmem] * (2 + len(parts)),
        out_specs=vmem,
        compiler_params=pltpu.CompilerParams(vmem_limit_bytes=16 * 2**20),
        cost_estimate=cost(4),
        name="feature_gradient",
    )(own, *parts, weight)


def join_kernel(*refs):
    out, at = refs[-1], 0
    for ref in refs[:-2]:
        out[pl.ds(at, ref.shape[0]), :] = ref[...]
        at += ref.shape[0]


def join_later(arrays, after):
    vmem = pl.BlockSpec(memory_space=pltpu.VMEM)
    length = sum(a.shape[0] for a in arrays)
    return pl.pallas_call(
        join_kernel,
        out_shape=jax.ShapeDtypeStruct((length, arrays[0].shape[1]), arrays[0].dtype),
        in_specs=[vmem] * len(arrays) + [pl.BlockSpec(memory_space=pl.ANY)],
        out_specs=vmem,
        compiler_params=pltpu.CompilerParams(vmem_limit_bytes=12 * 2**20),
        cost_estimate=cost(1),
        name="in_order",
    )(*arrays, after)


def same_later_kernel(*refs):
    del refs


def same_later(arrays, after):
    hbm = pl.BlockSpec(memory_space=pl.ANY)
    return pl.pallas_call(
        same_later_kernel,
        out_shape=[jax.ShapeDtypeStruct(a.shape, a.dtype) for a in arrays],
        in_specs=[hbm] * (len(arrays) + 1),
        out_specs=[hbm] * len(arrays),
        input_output_aliases={i: i for i in range(len(arrays))},
        cost_estimate=cost(1),
        name="in_order_in_place",
    )(*arrays, after)


def swap_cores(a):
    return lax.ppermute(a, "col", [(0, 1), (1, 0)])


def steps_along(a, axis, size):
    return [a] + [lax.ppermute(a, axis, [(i, (i + s) % size) for i in range(size)]) for s in range(1, size)]


def mark(*arrays):
    return jnp.concatenate([a.reshape(-1, a.shape[-1])[:8].astype(jnp.bfloat16) for a in arrays], axis=0)


def sum_of_eight(rows):
    rows = rows + lax.ppermute(rows, "z", [(i, i ^ 1) for i in range(8)])
    found = [rows] + [lax.ppermute(rows, "z", [(i, i ^ k) for i in range(8)]) for k in (2, 4, 6)]
    me = lax.div(lax.axis_index("z"), 2)
    total = None
    for pair in range(4):
        k = jnp.bitwise_xor(me, pair)
        part = jnp.where(k < 2, jnp.where(k == 0, found[0], found[1]), jnp.where(k == 2, found[2], found[3]))
        total = part if total is None else total + part
    return total


def sum_everywhere(term, c, after, before_last):
    n = term.shape[1]
    halves = term.reshape(2, 128, n)
    keep = lax.dynamic_index_in_dim(halves, c, 0, keepdims=False)
    give = lax.dynamic_index_in_dim(halves, 1 - c, 0, keepdims=False)
    half = join_later([keep + swap_cores(give)], after)
    rows = jnp.sum(lax.all_to_all(half.reshape(16, 8, n), PLANE, 0, 0, tiled=True), axis=0)
    rows = sum_of_eight(rows)
    rows = join_later([rows], before_last)
    half = lax.all_to_all(jnp.broadcast_to(rows[None], (16, 8, n)), PLANE, 0, 0, tiled=True).reshape(128, n)
    other = swap_cores(half)
    first = jnp.where(c == 0, half, other)
    second = jnp.where(c == 0, other, half)
    return jnp.concatenate([first, second], axis=0)


def local(features, weight, cotangent, tile_values, tile_rows, tile_cols, tile_count, send_blocks):
    width = features.shape[1]
    node_total = features.shape[0] * lax.axis_size("col") * lax.axis_size(DOM)
    c = lax.axis_index("col")
    z_me = lax.axis_index("z")
    r_me = lax.axis_index(PLANE)
    where = jnp.stack([c, z_me, r_me, lax.axis_index("y"), lax.axis_index("x")]).astype(jnp.int32)

    ids_row = jnp.pad(send_blocks.astype(jnp.bfloat16), ((0, META - 1), (0, width - send_blocks.shape[1])))
    feats = steps_along(jnp.concatenate([features, ids_row], axis=0), "z", 8)
    cot_mine = lax.all_gather(cotangent.reshape(4, BLK, width), PLANE, axis=0, tiled=True)
    packed = pack(tile_cols, tile_rows, tile_count, tile_values)
    sent = lax.all_to_all(packed, PLANE, 0, 0, tiled=True)

    meta = sent[:, 8 * BLK, :8].astype(jnp.int32).reshape(128)
    ids = jnp.stack([f[4 * BLK, :128] for f in feats]).astype(jnp.int32).reshape(8, 16, 8)
    ids = lax.dynamic_index_in_dim(ids, z_me, 2, keepdims=False).reshape(128)

    operands = (where, meta, ids, tile_cols, tile_rows, tile_count, sent)
    for_peer = swap_cores(hidden_parts(*operands, tile_values, feats))
    both = hidden_parts(*operands, tile_values, feats, for_peer)
    parts = lax.all_to_all(both.reshape(16, 4 * BLK, width), PLANE, 0, 0, tiled=True)
    [cot_mine] = same_later([cot_mine], mark(both))
    own, *away = grad_parts(*operands, cot_mine, swap_cores(cot_mine), tile_values)
    by_partition = (16, 4 * BLK, width)
    scale = float(1.0 / node_total**0.5)
    arrived = [
        lax.ppermute(part, "z", [(z, (z + step) % 8) for z in range(8)])
        for step, part in sorted(enumerate(away, 1), key=lambda e: -min(e[0], 8 - e[0]))
    ]
    term = weight_term(both.reshape(by_partition), cot_mine.reshape(by_partition), mark(arrived[0]), scale)
    feature_grad = feature_from(own, arrived, weight)
    output_rows = output_from(parts, weight)
    gate = join_later([mark(*arrived[:5])], parts)
    weight_grad = sum_everywhere(term, c, gate, mark(output_rows))
    return (output_rows, feature_grad, weight_grad)


def solution(mesh):
    grid = Mesh(mesh.devices.reshape(SIZES), ("y", "x", "z", "col"))
    every = ("y", "x", "z", "col")
    return jax.shard_map(
        local,
        mesh=grid,
        in_specs=(
            P(every, None),
            P(),
            P(every, None),
            P(every, None, None),
            P(every),
            P(every),
            P(every),
            P(every, None),
        ),
        out_specs=(P(every, None), P(every, None), P()),
        check_vma=False,
    )
```

```python
import functools

import jax
import jax.numpy as jnp
from jax import lax
from jax.experimental import pallas as pl
from jax.experimental.pallas import tpu as pltpu
from jax.sharding import Mesh
from jax.sharding import PartitionSpec as P

PLANE = ("y", "x")
DOM = ("y", "x", "z")
SIZES = (4, 4, 8, 2)
BLK = 128
META = 16


def pack_kernel(cols, rows, count, tiles, out):
    slots = out.shape[1] // BLK
    here = pl.ds(slots * BLK, META)
    lane = lax.broadcasted_iota(jnp.int32, (META, BLK), 1)
    line = lax.broadcasted_iota(jnp.int32, (META, BLK), 0)

    def clear(d, carry):
        out[d, here, :] = jnp.zeros((META, BLK), out.dtype)
        return carry

    lax.fori_loop(0, out.shape[0], clear, 0)

    def one(t, carry):
        @pl.when(cols[t] >= 4)
        def _():
            slot = jnp.maximum(cols[t] - 4, 0)
            d, z = lax.div(slot, slots), lax.rem(slot, slots)
            out[d, rows_at(z), :] = tiles[t]
            mark = jnp.where((lane == z) & (line == 0), rows[t] + 1, 0)
            out[d, here, :] = (out[d, here, :].astype(jnp.float32) + mark.astype(jnp.float32)).astype(out.dtype)

        return carry

    lax.fori_loop(0, count[0], one, 0)


def pack(cols, rows, count, tiles):
    groups, slots = 16, 8
    smem = pl.BlockSpec(memory_space=pltpu.SMEM)
    vmem = pl.BlockSpec(memory_space=pltpu.VMEM)
    return pl.pallas_call(
        pack_kernel,
        out_shape=jax.ShapeDtypeStruct((groups, slots * BLK + META, BLK), tiles.dtype),
        in_specs=[smem, smem, smem, vmem],
        out_specs=vmem,
        compiler_params=pltpu.CompilerParams(vmem_limit_bytes=12 * 2**20),
        cost_estimate=cost(3),
        name="pack_tiles",
    )(cols, rows, count, tiles)


def cost(us):
    return pl.CostEstimate(flops=us * 10**8, bytes_accessed=us * 3 * 10**6, transcendentals=0)


def rows_at(k):
    return pl.ds(pl.multiple_of(k * BLK, BLK), BLK)


def hidden_kernel(first, where, meta, ids, cols, rows, count, sent, tiles, *rest):
    feats, rest = rest[:8], rest[8:]
    out, total = rest[0], rest[-1]
    c, z_me, r_me = where[0], where[1], where[2]
    half = 1 - c if first else c

    def begin(i, carry):
        total[i] = jnp.zeros(total.shape[1:], total.dtype)
        return carry

    lax.fori_loop(0, total.shape[0], begin, 0)

    def add(tile, block, r, row):
        at = r * 4 + lax.rem(row, 4)
        total[at] = total[at] + jnp.dot(tile, block, preferred_element_type=jnp.float32)

    for s in range(8):
        z = jnp.bitwise_and(z_me - s + 8, 7)

        def remote(r, carry, s=s, z=z):
            mark = meta[r * 8 + z]

            @pl.when((mark > 0) & (lax.div(mark - 1, 4) == half))
            def _():
                add(sent[r, rows_at(z), :], feats[s][rows_at(ids[s * 16 + r]), :], r, mark - 1)

            return carry

        lax.fori_loop(0, 16, remote, 0, unroll=2)

    def own(t, carry):
        @pl.when((cols[t] < 4) & (lax.div(rows[t], 4) == half))
        def _():
            add(tiles[t], feats[0][rows_at(jnp.minimum(cols[t], 3)), :], r_me, rows[t])

        return carry

    lax.fori_loop(0, count[0], own, 0)

    def cast(i, carry):
        out[i] = total[i].astype(out.dtype)
        return carry

    if first:
        lax.fori_loop(0, total.shape[0], cast, 0)


def add_kernel(mine, arrived, out):
    def one(i, carry):
        out[i] = (mine[i] + arrived[i].astype(mine.dtype)).astype(out.dtype)
        return carry

    lax.fori_loop(0, mine.shape[0], one, 0)


def add_halves(mine, arrived):
    vmem = pl.BlockSpec(memory_space=pltpu.VMEM)
    return pl.pallas_call(
        add_kernel,
        out_shape=jax.ShapeDtypeStruct(arrived.shape, arrived.dtype),
        in_specs=[vmem] * 2,
        out_specs=vmem,
        compiler_params=pltpu.CompilerParams(vmem_limit_bytes=20 * 2**20),
        cost_estimate=cost(4),
        name="add_halves",
    )(mine, arrived)


def hidden_parts(first, where, meta, ids, cols, rows, count, sent, tiles, feats):
    smem = pl.BlockSpec(memory_space=pltpu.SMEM)
    vmem = pl.BlockSpec(memory_space=pltpu.VMEM)
    width = feats[0].shape[1]
    return pl.pallas_call(
        functools.partial(hidden_kernel, first),
        out_shape=jax.ShapeDtypeStruct((64, BLK, width), jnp.bfloat16 if first else jnp.float32),
        in_specs=[smem] * 6 + [vmem] * (2 + len(feats)),
        out_specs=vmem,
        scratch_shapes=[pltpu.VMEM((64, BLK, width), jnp.float32)] if first else [],
        compiler_params=pltpu.CompilerParams(vmem_limit_bytes=28 * 2**20),
        cost_estimate=cost(10),
        name="hidden_for_other_core" if first else "hidden_sums",
    )(where, meta, ids, cols, rows, count, sent, tiles, *feats)


def add_grads(where, meta, ids, cols, rows, count, sent, mine, peer, tiles, total):
    c, z_me, r_me = where[0], where[1], where[2]

    def add(at, tile, r, row):
        def go(cots):
            term = lax.dot_general(
                tile, cots[r * 4 + lax.rem(row, 4)], (((0,), (0,)), ((), ())), preferred_element_type=jnp.float32
            )
            total[at] = total[at] + term

        @pl.when(lax.div(row, 4) == c)
        def _():
            go(mine)

        @pl.when(lax.div(row, 4) != c)
        def _():
            go(peer)

    def remote(i, carry):
        r, z = lax.div(i, 8), lax.rem(i, 8)

        @pl.when(meta[i] > 0)
        def _():
            step, back = jnp.bitwise_and(z - z_me + 8, 7), jnp.bitwise_and(z_me - z + 8, 7)
            add(step * 4 + ids[back * 16 + r], sent[r, rows_at(z), :], r, meta[i] - 1)

        return carry

    lax.fori_loop(0, 128, remote, 0, unroll=4)

    def own(t, carry):
        @pl.when(cols[t] < 4)
        def _():
            add(jnp.minimum(cols[t], 3), tiles[t], r_me, rows[t])

        return carry

    lax.fori_loop(0, count[0], own, 0)


def grad_kernel(where, meta, ids, cols, rows, count, sent, mine, peer, tiles, *outs):
    total = outs[-1]

    def begin(i, carry):
        total[i] = jnp.zeros(total.shape[1:], total.dtype)
        return carry

    lax.fori_loop(0, total.shape[0], begin, 0)
    add_grads(where, meta, ids, cols, rows, count, sent, mine, peer, tiles, total)
    for k in range(4):
        outs[0][rows_at(k), :] = total[k]
    for step in range(1, 8):
        for k in range(4):
            outs[step][rows_at(k), :] = total[step * 4 + k].astype(outs[step].dtype)


def grad_parts(where, meta, ids, cols, rows, count, sent, mine, peer, tiles):
    smem = pl.BlockSpec(memory_space=pltpu.SMEM)
    vmem = pl.BlockSpec(memory_space=pltpu.VMEM)
    width = mine.shape[2]
    return pl.pallas_call(
        grad_kernel,
        out_shape=[jax.ShapeDtypeStruct((4 * BLK, width), jnp.float32)]
        + [jax.ShapeDtypeStruct((4 * BLK, width), jnp.bfloat16)] * 7,
        in_specs=[smem] * 6 + [vmem] * 4,
        out_specs=[vmem] * 8,
        scratch_shapes=[pltpu.VMEM((32, BLK, width), jnp.float32)],
        compiler_params=pltpu.CompilerParams(vmem_limit_bytes=28 * 2**20),
        cost_estimate=cost(8),
        name="grad_sums",
    )(where, meta, ids, cols, rows, count, sent, mine, peer, tiles)


def term_kernel(scale, parts, cots, after, term):
    del after
    term[...] = jnp.zeros(term.shape, term.dtype)

    def product(i, carry):
        term[...] += lax.dot_general(
            parts[i], cots[i], (((0,), (0,)), ((), ())), preferred_element_type=jnp.float32
        )
        return carry

    lax.fori_loop(0, parts.shape[0], product, 0)
    term[...] = term[...] * scale


def weight_term(parts, cots, after, scale):
    vmem = pl.BlockSpec(memory_space=pltpu.VMEM)
    width = parts.shape[2]
    return pl.pallas_call(
        functools.partial(term_kernel, scale),
        out_shape=jax.ShapeDtypeStruct((width, width), jnp.float32),
        in_specs=[vmem] * 2 + [pl.BlockSpec(memory_space=pl.ANY)],
        out_specs=vmem,
        compiler_params=pltpu.CompilerParams(vmem_limit_bytes=12 * 2**20),
        cost_estimate=cost(4),
        name="weight_term",
    )(parts, cots, after)


def output_kernel(parts, weight, *rest):
    output = rest[-1]
    total = parts[0].astype(jnp.float32)
    for i in range(1, parts.shape[0]):
        total = total + parts[i].astype(jnp.float32)
    hidden = total.astype(jnp.bfloat16)
    output[...] = jnp.dot(hidden, weight[...], preferred_element_type=jnp.float32).astype(output.dtype)


def output_from(parts, weight, *after):
    vmem = pl.BlockSpec(memory_space=pltpu.VMEM)
    return pl.pallas_call(
        output_kernel,
        out_shape=jax.ShapeDtypeStruct(parts.shape[1:], jnp.bfloat16),
        in_specs=[vmem] * 2 + [pl.BlockSpec(memory_space=pl.ANY)] * len(after),
        out_specs=vmem,
        compiler_params=pltpu.CompilerParams(vmem_limit_bytes=16 * 2**20),
        cost_estimate=cost(4),
        name="output_rows",
    )(parts, weight, *after)


def feature_kernel(own, *rest):
    weight, out = rest[-2:]
    total = own[...]
    for part in rest[:-2]:
        total = total + part[...].astype(jnp.float32)
    high = total.astype(jnp.bfloat16)
    low = (total - high.astype(jnp.float32)).astype(jnp.bfloat16)
    dims = (((1,), (1,)), ((), ()))
    grad = lax.dot_general(high, weight[...], dims, preferred_element_type=jnp.float32)
    grad = grad + lax.dot_general(low, weight[...], dims, preferred_element_type=jnp.float32)
    out[...] = grad.astype(out.dtype)


def feature_from(own, parts, weight):
    vmem = pl.BlockSpec(memory_space=pltpu.VMEM)
    return pl.pallas_call(
        feature_kernel,
        out_shape=jax.ShapeDtypeStruct(own.shape, jnp.bfloat16),
        in_specs=[vmem] * (2 + len(parts)),
        out_specs=vmem,
        compiler_params=pltpu.CompilerParams(vmem_limit_bytes=16 * 2**20),
        cost_estimate=cost(4),
        name="feature_gradient",
    )(own, *parts, weight)


def join_kernel(*refs):
    out, at = refs[-1], 0
    for ref in refs[:-2]:
        out[pl.ds(at, ref.shape[0]), :] = ref[...]
        at += ref.shape[0]


def join_later(arrays, after):
    vmem = pl.BlockSpec(memory_space=pltpu.VMEM)
    length = sum(a.shape[0] for a in arrays)
    return pl.pallas_call(
        join_kernel,
        out_shape=jax.ShapeDtypeStruct((length, arrays[0].shape[1]), arrays[0].dtype),
        in_specs=[vmem] * len(arrays) + [pl.BlockSpec(memory_space=pl.ANY)],
        out_specs=vmem,
        compiler_params=pltpu.CompilerParams(vmem_limit_bytes=12 * 2**20),
        cost_estimate=cost(1),
        name="in_order",
    )(*arrays, after)


def same_later_kernel(*refs):
    del refs


def same_later(arrays, after):
    hbm = pl.BlockSpec(memory_space=pl.ANY)
    return pl.pallas_call(
        same_later_kernel,
        out_shape=[jax.ShapeDtypeStruct(a.shape, a.dtype) for a in arrays],
        in_specs=[hbm] * (len(arrays) + 1),
        out_specs=[hbm] * len(arrays),
        input_output_aliases={i: i for i in range(len(arrays))},
        cost_estimate=cost(1),
        name="in_order_in_place",
    )(*arrays, after)


def swap_cores(a):
    return lax.ppermute(a, "col", [(0, 1), (1, 0)])


def steps_along(a, axis, size):
    return [a] + [lax.ppermute(a, axis, [(i, (i + s) % size) for i in range(size)]) for s in range(1, size)]


def mark(*arrays):
    return jnp.concatenate([a.reshape(-1, a.shape[-1])[:8].astype(jnp.bfloat16) for a in arrays], axis=0)


def sum_of_eight(rows):
    rows = rows + lax.ppermute(rows, "z", [(i, i ^ 1) for i in range(8)])
    found = [rows] + [lax.ppermute(rows, "z", [(i, i ^ k) for i in range(8)]) for k in (2, 4, 6)]
    me = lax.div(lax.axis_index("z"), 2)
    total = None
    for pair in range(4):
        k = jnp.bitwise_xor(me, pair)
        part = jnp.where(k < 2, jnp.where(k == 0, found[0], found[1]), jnp.where(k == 2, found[2], found[3]))
        total = part if total is None else total + part
    return total


def sum_everywhere(term, c, after, before_last):
    n = term.shape[1]
    halves = term.reshape(2, 128, n)
    keep = lax.dynamic_index_in_dim(halves, c, 0, keepdims=False)
    give = lax.dynamic_index_in_dim(halves, 1 - c, 0, keepdims=False)
    half = join_later([keep + swap_cores(give)], after)
    rows = jnp.sum(lax.all_to_all(half.reshape(16, 8, n), PLANE, 0, 0, tiled=True), axis=0)
    rows = sum_of_eight(rows)
    rows = join_later([rows], before_last)
    half = lax.all_to_all(jnp.broadcast_to(rows[None], (16, 8, n)), PLANE, 0, 0, tiled=True).reshape(128, n)
    other = swap_cores(half)
    first = jnp.where(c == 0, half, other)
    second = jnp.where(c == 0, other, half)
    return jnp.concatenate([first, second], axis=0)


def local(features, weight, cotangent, tile_values, tile_rows, tile_cols, tile_count, send_blocks):
    width = features.shape[1]
    node_total = features.shape[0] * lax.axis_size("col") * lax.axis_size(DOM)
    c = lax.axis_index("col")
    z_me = lax.axis_index("z")
    r_me = lax.axis_index(PLANE)
    where = jnp.stack([c, z_me, r_me, lax.axis_index("y"), lax.axis_index("x")]).astype(jnp.int32)

    ids_row = jnp.pad(send_blocks.astype(jnp.bfloat16), ((0, META - 1), (0, width - send_blocks.shape[1])))
    feats = steps_along(jnp.concatenate([features, ids_row], axis=0), "z", 8)
    cot_mine = lax.all_gather(cotangent.reshape(4, BLK, width), PLANE, axis=0, tiled=True)
    packed = pack(tile_cols, tile_rows, tile_count, tile_values)
    sent = lax.all_to_all(packed, PLANE, 0, 0, tiled=True)

    meta = sent[:, 8 * BLK, :8].astype(jnp.int32).reshape(128)
    ids = jnp.stack([f[4 * BLK, :128] for f in feats]).astype(jnp.int32).reshape(8, 16, 8)
    ids = lax.dynamic_index_in_dim(ids, z_me, 2, keepdims=False).reshape(128)

    operands = (where, meta, ids, tile_cols, tile_rows, tile_count, sent)
    for_peer = hidden_parts(True, *operands, tile_values, feats)
    both = add_halves(hidden_parts(False, *operands, tile_values, feats), swap_cores(for_peer))
    parts = lax.all_to_all(both.reshape(16, 4 * BLK, width), PLANE, 0, 0, tiled=True)
    [cot_mine] = same_later([cot_mine], mark(both))
    own, *away = grad_parts(*operands, cot_mine, swap_cores(cot_mine), tile_values)
    by_partition = (16, 4 * BLK, width)
    scale = float(1.0 / node_total**0.5)
    arrived = [
        lax.ppermute(part, "z", [(z, (z + step) % 8) for z in range(8)])
        for step, part in sorted(enumerate(away, 1), key=lambda e: -min(e[0], 8 - e[0]))
    ]
    term = weight_term(both.reshape(by_partition), cot_mine.reshape(by_partition), mark(arrived[0]), scale)
    feature_grad = feature_from(own, arrived, weight)
    output_rows = output_from(parts, weight)
    gate = join_later([mark(*arrived[:5])], parts)
    weight_grad = sum_everywhere(term, c, gate, mark(output_rows))
    return (output_rows, feature_grad, weight_grad)


def solution(mesh):
    grid = Mesh(mesh.devices.reshape(SIZES), ("y", "x", "z", "col"))
    every = ("y", "x", "z", "col")
    return jax.shard_map(
        local,
        mesh=grid,
        in_specs=(
            P(every, None),
            P(),
            P(every, None),
            P(every, None, None),
            P(every),
            P(every),
            P(every),
            P(every, None),
        ),
        out_specs=(P(every, None), P(every, None), P()),
        check_vma=False,
    )
```

```python
import functools

import jax
import jax.numpy as jnp
from jax import lax
from jax.experimental import pallas as pl
from jax.experimental.pallas import tpu as pltpu
from jax.sharding import Mesh
from jax.sharding import PartitionSpec as P

PLANE = ("y", "x")
DOM = ("y", "x", "z")
SIZES = (4, 4, 8, 2)
BLK = 128
META = 16


def pack_kernel(cols, rows, count, tiles, out):
    slots = out.shape[1] // BLK
    here = pl.ds(slots * BLK, META)
    lane = lax.broadcasted_iota(jnp.int32, (META, BLK), 1)
    line = lax.broadcasted_iota(jnp.int32, (META, BLK), 0)

    def clear(d, carry):
        out[d, here, :] = jnp.zeros((META, BLK), out.dtype)
        return carry

    lax.fori_loop(0, out.shape[0], clear, 0)

    def one(t, carry):
        @pl.when(cols[t] >= 4)
        def _():
            slot = jnp.maximum(cols[t] - 4, 0)
            d, z = lax.div(slot, slots), lax.rem(slot, slots)
            out[d, rows_at(z), :] = tiles[t]
            mark = jnp.where((lane == z) & (line == 0), rows[t] + 1, 0)
            out[d, here, :] = (out[d, here, :].astype(jnp.float32) + mark.astype(jnp.float32)).astype(out.dtype)

        return carry

    lax.fori_loop(0, count[0], one, 0)


def pack(cols, rows, count, tiles):
    groups, slots = 16, 8
    smem = pl.BlockSpec(memory_space=pltpu.SMEM)
    vmem = pl.BlockSpec(memory_space=pltpu.VMEM)
    return pl.pallas_call(
        pack_kernel,
        out_shape=jax.ShapeDtypeStruct((groups, slots * BLK + META, BLK), tiles.dtype),
        in_specs=[smem, smem, smem, vmem],
        out_specs=vmem,
        compiler_params=pltpu.CompilerParams(vmem_limit_bytes=12 * 2**20),
        cost_estimate=cost(3),
        name="pack_tiles",
    )(cols, rows, count, tiles)


def cost(us):
    return pl.CostEstimate(flops=us * 10**8, bytes_accessed=us * 3 * 10**6, transcendentals=0)


def rows_at(k):
    return pl.ds(pl.multiple_of(k * BLK, BLK), BLK)


def hidden_kernel(first, where, meta, ids, cols, rows, count, sent, tiles, *rest):
    feats, rest = rest[:8], rest[8:]
    out, total = rest[0], rest[-1]
    c, z_me, r_me = where[0], where[1], where[2]
    half = 1 - c if first else c

    def begin(i, carry):
        total[i] = jnp.zeros(total.shape[1:], total.dtype)
        return carry

    lax.fori_loop(0, total.shape[0], begin, 0, unroll=4)

    def add(tile, block, r, row):
        at = r * 4 + lax.rem(row, 4)
        total[at] = total[at] + jnp.dot(tile, block, preferred_element_type=jnp.float32)

    for s in range(8):
        z = jnp.bitwise_and(z_me - s + 8, 7)

        def remote(r, carry, s=s, z=z):
            mark = meta[r * 8 + z]

            @pl.when((mark > 0) & (lax.div(mark - 1, 4) == half))
            def _():
                add(sent[r, rows_at(z), :], feats[s][rows_at(ids[s * 16 + r]), :], r, mark - 1)

            return carry

        lax.fori_loop(0, 16, remote, 0, unroll=2)

    def own(t, carry):
        @pl.when((cols[t] < 4) & (lax.div(rows[t], 4) == half))
        def _():
            add(tiles[t], feats[0][rows_at(jnp.minimum(cols[t], 3)), :], r_me, rows[t])

        return carry

    lax.fori_loop(0, count[0], own, 0)

    def cast(i, carry):
        out[i] = total[i].astype(out.dtype)
        return carry

    if first:
        lax.fori_loop(0, total.shape[0], cast, 0, unroll=4)


def add_kernel(mine, arrived, out):
    def one(i, carry):
        out[i] = (mine[i] + arrived[i].astype(mine.dtype)).astype(out.dtype)
        return carry

    lax.fori_loop(0, mine.shape[0], one, 0, unroll=4)


def add_halves(mine, arrived):
    vmem = pl.BlockSpec(memory_space=pltpu.VMEM)
    return pl.pallas_call(
        add_kernel,
        out_shape=jax.ShapeDtypeStruct(arrived.shape, arrived.dtype),
        in_specs=[vmem] * 2,
        out_specs=vmem,
        compiler_params=pltpu.CompilerParams(vmem_limit_bytes=20 * 2**20),
        cost_estimate=cost(4),
        name="add_halves",
    )(mine, arrived)


def hidden_parts(first, where, meta, ids, cols, rows, count, sent, tiles, feats):
    smem = pl.BlockSpec(memory_space=pltpu.SMEM)
    vmem = pl.BlockSpec(memory_space=pltpu.VMEM)
    width = feats[0].shape[1]
    return pl.pallas_call(
        functools.partial(hidden_kernel, first),
        out_shape=jax.ShapeDtypeStruct((64, BLK, width), jnp.bfloat16 if first else jnp.float32),
        in_specs=[smem] * 6 + [vmem] * (2 + len(feats)),
        out_specs=vmem,
        scratch_shapes=[pltpu.VMEM((64, BLK, width), jnp.float32)] if first else [],
        compiler_params=pltpu.CompilerParams(vmem_limit_bytes=28 * 2**20),
        cost_estimate=cost(10),
        name="hidden_for_other_core" if first else "hidden_sums",
    )(where, meta, ids, cols, rows, count, sent, tiles, *feats)


def add_grads(where, meta, ids, cols, rows, count, sent, mine, peer, tiles, total):
    c, z_me, r_me = where[0], where[1], where[2]

    def add(at, tile, r, row):
        def go(cots):
            term = lax.dot_general(
                tile, cots[r * 4 + lax.rem(row, 4)], (((0,), (0,)), ((), ())), preferred_element_type=jnp.float32
            )
            total[at] = total[at] + term

        @pl.when(lax.div(row, 4) == c)
        def _():
            go(mine)

        @pl.when(lax.div(row, 4) != c)
        def _():
            go(peer)

    def remote(i, carry):
        r, z = lax.div(i, 8), lax.rem(i, 8)

        @pl.when(meta[i] > 0)
        def _():
            step, back = jnp.bitwise_and(z - z_me + 8, 7), jnp.bitwise_and(z_me - z + 8, 7)
            add(step * 4 + ids[back * 16 + r], sent[r, rows_at(z), :], r, meta[i] - 1)

        return carry

    lax.fori_loop(0, 128, remote, 0, unroll=4)

    def own(t, carry):
        @pl.when(cols[t] < 4)
        def _():
            add(jnp.minimum(cols[t], 3), tiles[t], r_me, rows[t])

        return carry

    lax.fori_loop(0, count[0], own, 0)


def grad_kernel(where, meta, ids, cols, rows, count, sent, mine, peer, tiles, *outs):
    total = outs[-1]

    def begin(i, carry):
        total[i] = jnp.zeros(total.shape[1:], total.dtype)
        return carry

    lax.fori_loop(0, total.shape[0], begin, 0, unroll=4)
    add_grads(where, meta, ids, cols, rows, count, sent, mine, peer, tiles, total)
    for k in range(4):
        outs[0][rows_at(k), :] = total[k]
    for step in range(1, 8):
        for k in range(4):
            outs[step][rows_at(k), :] = total[step * 4 + k].astype(outs[step].dtype)


def grad_parts(where, meta, ids, cols, rows, count, sent, mine, peer, tiles):
    smem = pl.BlockSpec(memory_space=pltpu.SMEM)
    vmem = pl.BlockSpec(memory_space=pltpu.VMEM)
    width = mine.shape[2]
    return pl.pallas_call(
        grad_kernel,
        out_shape=[jax.ShapeDtypeStruct((4 * BLK, width), jnp.float32)]
        + [jax.ShapeDtypeStruct((4 * BLK, width), jnp.bfloat16)] * 7,
        in_specs=[smem] * 6 + [vmem] * 4,
        out_specs=[vmem] * 8,
        scratch_shapes=[pltpu.VMEM((32, BLK, width), jnp.float32)],
        compiler_params=pltpu.CompilerParams(vmem_limit_bytes=28 * 2**20),
        cost_estimate=cost(8),
        name="grad_sums",
    )(where, meta, ids, cols, rows, count, sent, mine, peer, tiles)


def term_kernel(scale, parts, cots, after, term):
    del after
    term[...] = jnp.zeros(term.shape, term.dtype)

    def product(i, carry):
        term[...] += lax.dot_general(
            parts[i], cots[i], (((0,), (0,)), ((), ())), preferred_element_type=jnp.float32
        )
        return carry

    lax.fori_loop(0, parts.shape[0], product, 0)
    term[...] = term[...] * scale


def weight_term(parts, cots, after, scale):
    vmem = pl.BlockSpec(memory_space=pltpu.VMEM)
    width = parts.shape[2]
    return pl.pallas_call(
        functools.partial(term_kernel, scale),
        out_shape=jax.ShapeDtypeStruct((width, width), jnp.float32),
        in_specs=[vmem] * 2 + [pl.BlockSpec(memory_space=pl.ANY)],
        out_specs=vmem,
        compiler_params=pltpu.CompilerParams(vmem_limit_bytes=12 * 2**20),
        cost_estimate=cost(4),
        name="weight_term",
    )(parts, cots, after)


def output_kernel(parts, weight, *rest):
    output = rest[-1]
    total = parts[0].astype(jnp.float32)
    for i in range(1, parts.shape[0]):
        total = total + parts[i].astype(jnp.float32)
    hidden = total.astype(jnp.bfloat16)
    output[...] = jnp.dot(hidden, weight[...], preferred_element_type=jnp.float32).astype(output.dtype)


def output_from(parts, weight, *after):
    vmem = pl.BlockSpec(memory_space=pltpu.VMEM)
    return pl.pallas_call(
        output_kernel,
        out_shape=jax.ShapeDtypeStruct(parts.shape[1:], jnp.bfloat16),
        in_specs=[vmem] * 2 + [pl.BlockSpec(memory_space=pl.ANY)] * len(after),
        out_specs=vmem,
        compiler_params=pltpu.CompilerParams(vmem_limit_bytes=16 * 2**20),
        cost_estimate=cost(4),
        name="output_rows",
    )(parts, weight, *after)


def feature_kernel(own, *rest):
    weight, out = rest[-2:]
    total = own[...]
    for part in rest[:-2]:
        total = total + part[...].astype(jnp.float32)
    high = total.astype(jnp.bfloat16)
    low = (total - high.astype(jnp.float32)).astype(jnp.bfloat16)
    dims = (((1,), (1,)), ((), ()))
    grad = lax.dot_general(high, weight[...], dims, preferred_element_type=jnp.float32)
    grad = grad + lax.dot_general(low, weight[...], dims, preferred_element_type=jnp.float32)
    out[...] = grad.astype(out.dtype)


def feature_from(own, parts, weight):
    vmem = pl.BlockSpec(memory_space=pltpu.VMEM)
    return pl.pallas_call(
        feature_kernel,
        out_shape=jax.ShapeDtypeStruct(own.shape, jnp.bfloat16),
        in_specs=[vmem] * (2 + len(parts)),
        out_specs=vmem,
        compiler_params=pltpu.CompilerParams(vmem_limit_bytes=16 * 2**20),
        cost_estimate=cost(4),
        name="feature_gradient",
    )(own, *parts, weight)


def join_kernel(*refs):
    out, at = refs[-1], 0
    for ref in refs[:-2]:
        out[pl.ds(at, ref.shape[0]), :] = ref[...]
        at += ref.shape[0]


def join_later(arrays, after):
    vmem = pl.BlockSpec(memory_space=pltpu.VMEM)
    length = sum(a.shape[0] for a in arrays)
    return pl.pallas_call(
        join_kernel,
        out_shape=jax.ShapeDtypeStruct((length, arrays[0].shape[1]), arrays[0].dtype),
        in_specs=[vmem] * len(arrays) + [pl.BlockSpec(memory_space=pl.ANY)],
        out_specs=vmem,
        compiler_params=pltpu.CompilerParams(vmem_limit_bytes=12 * 2**20),
        cost_estimate=cost(1),
        name="in_order",
    )(*arrays, after)


def same_later_kernel(*refs):
    del refs


def same_later(arrays, after):
    hbm = pl.BlockSpec(memory_space=pl.ANY)
    return pl.pallas_call(
        same_later_kernel,
        out_shape=[jax.ShapeDtypeStruct(a.shape, a.dtype) for a in arrays],
        in_specs=[hbm] * (len(arrays) + 1),
        out_specs=[hbm] * len(arrays),
        input_output_aliases={i: i for i in range(len(arrays))},
        cost_estimate=cost(1),
        name="in_order_in_place",
    )(*arrays, after)


def swap_cores(a):
    return lax.ppermute(a, "col", [(0, 1), (1, 0)])


def steps_along(a, axis, size):
    return [a] + [lax.ppermute(a, axis, [(i, (i + s) % size) for i in range(size)]) for s in range(1, size)]


def mark(*arrays):
    return jnp.concatenate([a.reshape(-1, a.shape[-1])[:8].astype(jnp.bfloat16) for a in arrays], axis=0)


def sum_of_eight(rows):
    rows = rows + lax.ppermute(rows, "z", [(i, i ^ 1) for i in range(8)])
    found = [rows] + [lax.ppermute(rows, "z", [(i, i ^ k) for i in range(8)]) for k in (2, 4, 6)]
    me = lax.div(lax.axis_index("z"), 2)
    total = None
    for pair in range(4):
        k = jnp.bitwise_xor(me, pair)
        part = jnp.where(k < 2, jnp.where(k == 0, found[0], found[1]), jnp.where(k == 2, found[2], found[3]))
        total = part if total is None else total + part
    return total


def sum_everywhere(term, c, after, before_last):
    n = term.shape[1]
    halves = term.reshape(2, 128, n)
    keep = lax.dynamic_index_in_dim(halves, c, 0, keepdims=False)
    give = lax.dynamic_index_in_dim(halves, 1 - c, 0, keepdims=False)
    half = join_later([keep + swap_cores(give)], after)
    rows = jnp.sum(lax.all_to_all(half.reshape(16, 8, n), PLANE, 0, 0, tiled=True), axis=0)
    rows = sum_of_eight(rows)
    rows = join_later([rows], before_last)
    half = lax.all_to_all(jnp.broadcast_to(rows[None], (16, 8, n)), PLANE, 0, 0, tiled=True).reshape(128, n)
    other = swap_cores(half)
    first = jnp.where(c == 0, half, other)
    second = jnp.where(c == 0, other, half)
    return jnp.concatenate([first, second], axis=0)


def local(features, weight, cotangent, tile_values, tile_rows, tile_cols, tile_count, send_blocks):
    width = features.shape[1]
    node_total = features.shape[0] * lax.axis_size("col") * lax.axis_size(DOM)
    c = lax.axis_index("col")
    z_me = lax.axis_index("z")
    r_me = lax.axis_index(PLANE)
    where = jnp.stack([c, z_me, r_me, lax.axis_index("y"), lax.axis_index("x")]).astype(jnp.int32)

    ids_row = jnp.pad(send_blocks.astype(jnp.bfloat16), ((0, META - 1), (0, width - send_blocks.shape[1])))
    feats = steps_along(jnp.concatenate([features, ids_row], axis=0), "z", 8)
    cot_mine = lax.all_gather(cotangent.reshape(4, BLK, width), PLANE, axis=0, tiled=True)
    packed = pack(tile_cols, tile_rows, tile_count, tile_values)
    sent = lax.all_to_all(packed, PLANE, 0, 0, tiled=True)

    meta = sent[:, 8 * BLK, :8].astype(jnp.int32).reshape(128)
    ids = jnp.stack([f[4 * BLK, :128] for f in feats]).astype(jnp.int32).reshape(8, 16, 8)
    ids = lax.dynamic_index_in_dim(ids, z_me, 2, keepdims=False).reshape(128)

    operands = (where, meta, ids, tile_cols, tile_rows, tile_count, sent)
    for_peer = hidden_parts(True, *operands, tile_values, feats)
    both = add_halves(hidden_parts(False, *operands, tile_values, feats), swap_cores(for_peer))
    parts = lax.all_to_all(both.reshape(16, 4 * BLK, width), PLANE, 0, 0, tiled=True)
    [cot_mine] = same_later([cot_mine], both)
    own, *away = grad_parts(*operands, cot_mine, swap_cores(cot_mine), tile_values)
    by_partition = (16, 4 * BLK, width)
    scale = float(1.0 / node_total**0.5)
    arrived = [
        lax.ppermute(part, "z", [(z, (z + step) % 8) for z in range(8)])
        for step, part in sorted(enumerate(away, 1), key=lambda e: -min(e[0], 8 - e[0]))
    ]
    term = weight_term(both.reshape(by_partition), cot_mine.reshape(by_partition), mark(arrived[0]), scale)
    feature_grad = feature_from(own, arrived, weight)
    output_rows = output_from(parts, weight)
    gate = join_later([mark(*arrived[:5])], parts)
    weight_grad = sum_everywhere(term, c, gate, mark(output_rows))
    return (output_rows, feature_grad, weight_grad)


def solution(mesh):
    grid = Mesh(mesh.devices.reshape(SIZES), ("y", "x", "z", "col"))
    every = ("y", "x", "z", "col")
    return jax.shard_map(
        local,
        mesh=grid,
        in_specs=(
            P(every, None),
            P(),
            P(every, None),
            P(every, None, None),
            P(every),
            P(every),
            P(every),
            P(every, None),
        ),
        out_specs=(P(every, None), P(every, None), P()),
        check_vma=False,
    )
```
